32 devices in a mesh: pos: 8 (over y, x, core), obj: 4 (over z).
Axes of the slice: x: 2, y: 2, z: 4, core: 2. Of those that a mesh axis runs over, the one named last changes fastest.
Arguments:
- object_field: float32 [2, 2048, 3072], P(None, 'obj', 'pos'), may hold values from -5 to 5
- probe: float32 [2, 256, 256], replicated, may hold values from -5 to 5
- amplitude: bfloat16 [512, 256, 256], P(('pos', 'obj')), may hold values from 0.19921875 to 3
- row_offset: int32 [512], P(('pos', 'obj')), may hold values from 0 to 256
- col_offset: int32 [512], P(('pos', 'obj')), may hold values from 0 to 128
- owner: int32 [512], P(('pos', 'obj')), may hold values from 0 to 7, as said below
Outputs:
- new_object: float32 [2, 2048, 3072], P(None, 'obj', 'pos')
- new_probe: float32 [2, 256, 256], replicated
The draws below stay inside these ranges and needn't reach their ends.
Inputs may be any that keep to these rules, and one draw needn't show every extreme that they name: Among the 16 positions of one device no owner is named more than 3 times; in each row band one owner is named exactly 3 times by every device.
All inputs are finite; a program needn't handle non-finite values.
Results may differ from the reference program's by a relative error of at most 0.005.
The reference program's roundings to bfloat16 on the way count: a program that leaves them out, or rounds other values in their place, can miss the bound.
Values may be sent and summed in bfloat16 or wider, within the bound.
No kernel may reach another device: no remote copies, remote signals or barrier semaphores. Data moves between devices by JAX's collectives and lax.ppermute only.
A program may use at most 128 MiB of HBM per device.

```python
import math
import jax
import jax.numpy as jnp
from jax import lax

PATCH = 256
TILE_ROWS = 512
TILE_COLS = 384
POS_DEV = 16
CAPACITY = 3
NPOS = 512
OBJ_ROWS = 2048
OBJ_COLS = 3072
N_POS = 8
N_OBJ = 4


def draw_owner(key, part):
    count = N_POS * N_OBJ
    hottest = jax.random.randint(jax.random.fold_in(key, 1), (N_OBJ,), 0, N_POS)
    block_keys = jax.random.split(jax.random.fold_in(key, 2), count)
    band = jnp.arange(count) % N_OBJ

    def one_block(block_key, hot_owner):
        first, second = jax.random.split(block_key)
        spare = jax.random.permutation(first, (N_POS - 1) * CAPACITY)[:POS_DEV - CAPACITY]
        others = (hot_owner + 1 + spare // CAPACITY) % N_POS
        listed = jnp.concatenate([jnp.full((CAPACITY,), hot_owner, jnp.int32), others.astype(jnp.int32)])
        order = jax.random.permutation(second, POS_DEV)
        return listed[order]
    return jax.vmap(one_block)(block_keys, hottest[band]).reshape(-1).astype(jnp.int32)


def plant(entries, stream_key, smallest, high):
    shape = entries.shape
    spot = [jax.random.randint(jax.random.fold_in(stream_key, axis), (), 0, shape[axis]) for axis in range(len(shape))]
    entries = entries.at[tuple(spot)].set(smallest)
    longest = shape.index(max(shape))
    spot[longest] = (spot[longest] + 1) % shape[longest]
    return entries.at[tuple(spot)].set(high)


def level_of(stream_key, dims, pieces, low, top_value):
    gain = 1.0
    for dim, shards_of in pieces:
        steps = jax.random.uniform(jax.random.fold_in(jax.random.fold_in(stream_key, 6), dim), (shards_of,), jnp.float32, low / len(pieces), top_value / len(pieces))
        gain = gain * jnp.repeat(jnp.exp(steps), dims[dim] // shards_of).reshape((-1,) + (1,) * (len(dims) - 1 - dim))
    return gain


def noise(key, shape, spread, limit, pieces=(), held_as=jnp.bfloat16):
    values = spread * jax.random.normal(key, shape, jnp.float32)
    if pieces:
        values = values * level_of(key, shape, pieces, -0.22, 0.18)
    return jnp.clip(values, -limit, limit).astype(held_as)


def setup_inputs(seed: int = 0) -> dict:
    streams_of = jax.random.split(jax.random.key(seed), 7)
    return {
        "object_field": noise(streams_of[0], (2, OBJ_ROWS, OBJ_COLS), 0.7, 5.0, ((1, 4), (2, 8)), jnp.float32),
        "probe": noise(streams_of[1], (2, PATCH, PATCH), 0.7, 5.0, (), jnp.float32),
        "amplitude": jnp.clip(jnp.exp(math.log(3.0) - 2.7119641 * jax.random.uniform(streams_of[2], (NPOS, PATCH, PATCH), jnp.float32) ** level_of(streams_of[2], (NPOS, PATCH, PATCH), ((0, 32),), -0.2, 0.2)), 0.19921875, 3.0).astype(jnp.bfloat16),
        "row_offset": plant(jax.random.randint(streams_of[3], (NPOS,), 0, TILE_ROWS - PATCH + 1), jax.random.fold_in(streams_of[3], 1), 0, TILE_ROWS - PATCH).astype(jnp.int32),
        "col_offset": plant(jax.random.randint(streams_of[4], (NPOS,), 0, TILE_COLS - PATCH + 1), jax.random.fold_in(streams_of[4], 1), 0, TILE_COLS - PATCH).astype(jnp.int32),
        "owner": draw_owner(jax.random.fold_in(streams_of[6], 71), 0),
    }


def dft_tables(size):
    index = jnp.arange(size, dtype=jnp.int32)
    product = index[:, None] * index[None, :] % size
    angle = product.astype(jnp.float32) * (2.0 * math.pi / size)
    scale = 1.0 / math.sqrt(size)
    real_part = (jnp.cos(angle) * scale).astype(jnp.bfloat16)
    imag_part = (-jnp.sin(angle) * scale).astype(jnp.bfloat16)
    return (real_part, imag_part)

def left_apply(mat_re, mat_im, val_re, val_im):

    def product(matrix, values):
        return jnp.einsum('jk,bkl->bjl', matrix.astype(jnp.float32), values.astype(jnp.float32), precision=lax.Precision.HIGHEST)
    return (product(mat_re, val_re) - product(mat_im, val_im), product(mat_re, val_im) + product(mat_im, val_re))

def right_apply(val_re, val_im, mat_re, mat_im):

    def product(values, matrix):
        return jnp.einsum('bjk,kl->bjl', values.astype(jnp.float32), matrix.astype(jnp.float32), precision=lax.Precision.HIGHEST)
    return (product(val_re, mat_re) - product(val_im, mat_im), product(val_re, mat_im) + product(val_im, mat_re))

def position_terms(patches, amps, probe, four_re, four_im, conj_im):
    patch_re = patches[:, 0].astype(jnp.float32)
    patch_im = patches[:, 1].astype(jnp.float32)
    probe_re = probe[0]
    probe_im = probe[1]
    psi_re = (probe_re * patch_re - probe_im * patch_im).astype(jnp.bfloat16)
    psi_im = (probe_re * patch_im + probe_im * patch_re).astype(jnp.bfloat16)
    left_re, left_im = left_apply(four_re, four_im, psi_re, psi_im)
    wave_re, wave_im = right_apply(left_re.astype(jnp.bfloat16), left_im.astype(jnp.bfloat16), four_re, four_im)
    magnitude = jnp.sqrt(wave_re * wave_re + wave_im * wave_im)
    factor = 1.0 - amps.astype(jnp.float32) / jnp.maximum(magnitude, 0.5)
    diff_re = (wave_re * factor).astype(jnp.bfloat16)
    diff_im = (wave_im * factor).astype(jnp.bfloat16)
    back_re, back_im = left_apply(four_re, conj_im, diff_re, diff_im)
    chi_re, chi_im = right_apply(back_re.astype(jnp.bfloat16), back_im.astype(jnp.bfloat16), four_re, conj_im)
    grad_re = (probe_re * chi_re + probe_im * chi_im).astype(jnp.bfloat16)
    grad_im = (probe_re * chi_im - probe_im * chi_re).astype(jnp.bfloat16)
    term_re = lax.optimization_barrier(jnp.sum(patch_re * chi_re + patch_im * chi_im, axis=0))
    term_im = lax.optimization_barrier(jnp.sum(patch_re * chi_im - patch_im * chi_re, axis=0))
    return (jnp.stack([grad_re, grad_im], axis=1), jnp.stack([term_re, term_im]))

def reference(object_field, probe, amplitude, row_offset, col_offset, owner):
    npos = amplitude.shape[0]
    size = amplitude.shape[1]
    index = jnp.arange(npos, dtype=jnp.int32)
    band = index // POS_DEV % N_OBJ
    rows = (band * TILE_ROWS + row_offset).astype(jnp.int32)
    cols = (owner * TILE_COLS + col_offset).astype(jnp.int32)
    four_re, four_im = dft_tables(size)
    conj_im = -four_im
    zero = jnp.zeros((), jnp.int32)

    def step(carry, block):
        grad_obj, probe_acc = carry
        start = (block * POS_DEV).astype(jnp.int32)
        row_here = lax.dynamic_slice_in_dim(rows, start, POS_DEV, 0)
        col_here = lax.dynamic_slice_in_dim(cols, start, POS_DEV, 0)
        patches = jax.vmap(lambda row, col: lax.dynamic_slice(object_field, (zero, row, col), (2, size, size)))(row_here, col_here).astype(jnp.bfloat16)
        amps = lax.dynamic_slice_in_dim(amplitude, start, POS_DEV, 0)
        grads, term = position_terms(patches, amps, probe, four_re, four_im, conj_im)

        def add_one(item, acc):
            corner = (zero, row_here[item], col_here[item])
            window = lax.dynamic_slice(acc, corner, (2, size, size))
            return lax.dynamic_update_slice(acc, window + grads[item].astype(jnp.float32), corner)
        grad_obj = lax.fori_loop(0, POS_DEV, add_one, grad_obj)
        return ((grad_obj, probe_acc + term), None)
    blocks = jnp.arange(npos // POS_DEV, dtype=jnp.int32)
    start_carry = (jnp.zeros(object_field.shape, jnp.float32), jnp.zeros(probe.shape, jnp.float32))
    (object_grad, probe_grad), _ = lax.scan(step, start_carry, blocks)
    smooth = 4.0 * object_field - jnp.roll(object_field, 1, 1) - jnp.roll(object_field, -1, 1)
    smooth = smooth - jnp.roll(object_field, 1, 2) - jnp.roll(object_field, -1, 2)
    new_object = object_field - 0.25 * (object_grad + 0.5 * smooth)
    new_probe = probe - probe_grad * (1.0 / math.sqrt(npos))
    return (new_object, new_probe)
```

```python
import functools
import math

import jax
import jax.numpy as jnp
import numpy as np
from jax import lax
from jax.experimental import pallas as pl
from jax.experimental.pallas import tpu as pltpu
from jax.sharding import PartitionSpec as P

LANES = 128
INFO_ROWS = 16
VMEM_LIMIT = 56 * 2**20
bf16 = jnp.bfloat16
f32 = jnp.float32


def dft_blocks(size):
    index = np.arange(size, dtype=np.int32)
    product = index[:, None] * index[None, :] % size
    angle = product.astype(np.float32) * np.float32(2.0 * math.pi / size)
    scale = np.float32(1.0 / math.sqrt(size))
    real_part = (np.cos(angle) * scale).astype(bf16)
    imag_part = (-np.sin(angle) * scale).astype(bf16)
    left = np.block([[real_part, -imag_part], [imag_part, real_part]])
    right = np.block([[real_part, imag_part], [-imag_part, real_part]])
    return left, right


def exchange(value, axis, distance):
    count = lax.axis_size(axis)
    return lax.ppermute(value, axis, [(i, i ^ distance) for i in range(count)])


def dot(a, b):
    return jnp.dot(a, b, preferred_element_type=f32)


def pack_kernel(n_pos, capacity, pos_dev, size, me_ref, owner, row, col, amp, *rest):
    outs = rest[:n_pos]
    counts, source, info, sems, info_sems = rest[n_pos:]
    me = me_ref[0]
    for q in range(n_pos):
        counts[q] = 0
    for item in range(pos_dev):
        who = owner[item]
        rank = counts[who]
        source[who * capacity + rank] = item
        counts[who] = rank + 1
    lane = lax.broadcasted_iota(jnp.int32, (INFO_ROWS, size), 1)
    copies = []
    for d in range(n_pos):
        partner = jnp.bitwise_xor(me, d)
        held = counts[partner]
        block = jnp.zeros((INFO_ROWS, size), f32)
        for k in range(capacity):
            valid = k < held
            item = jnp.where(valid, source[partner * capacity + k], 0)
            copy = pltpu.make_async_copy(amp.at[item], outs[d].at[pl.ds(k * size, size)], sems.at[d, k])
            pl.when(valid)(copy.start)
            copies.append((valid, copy))
            numbers = (jnp.where(valid, row[item], 0), jnp.where(valid, col[item], 0), valid.astype(jnp.int32))
            for j, number in enumerate(numbers):
                block = jnp.where(lane == 3 * k + j, number.astype(f32), block)
        info[d] = block.astype(bf16)
        copy = pltpu.make_async_copy(info.at[d], outs[d].at[pl.ds(capacity * size, INFO_ROWS)], info_sems.at[d])
        copy.start()
        copies.append((None, copy))
    for valid, copy in copies:
        if valid is None:
            copy.wait()
        else:
            pl.when(valid)(copy.wait)


def pack(me, owner, row, col, amplitude, n_pos, capacity):
    pos_dev, size, _ = amplitude.shape
    smem = pl.BlockSpec(memory_space=pltpu.SMEM)
    hbm = pl.BlockSpec(memory_space=pl.ANY)
    rows = capacity * size + INFO_ROWS
    return pl.pallas_call(
        functools.partial(pack_kernel, n_pos, capacity, pos_dev, size),
        in_specs=[smem, smem, smem, smem, hbm],
        out_specs=[hbm] * n_pos,
        out_shape=[jax.ShapeDtypeStruct((rows, size), bf16)] * n_pos,
        scratch_shapes=[
            pltpu.SMEM((n_pos,), jnp.int32),
            pltpu.SMEM((n_pos * capacity,), jnp.int32),
            pltpu.VMEM((n_pos, INFO_ROWS, size), bf16),
            pltpu.SemaphoreType.DMA((n_pos, capacity)),
            pltpu.SemaphoreType.DMA((n_pos,)),
        ],
        compiler_params=pltpu.CompilerParams(vmem_limit_bytes=16 * 2**20),
        name="pack",
    )(me, owner, row, col, amplitude)


def prepare_kernel(parts, tile, out):
    for plane in range(2):
        for k in range(parts):
            block = tile[plane, :, k * LANES : (k + 1) * LANES]
            out[plane * parts + k] = block.astype(bf16).astype(f32)


def prepare(tile):
    _, rows, cols = tile.shape
    parts = cols // LANES
    return pl.pallas_call(
        functools.partial(prepare_kernel, parts),
        out_shape=jax.ShapeDtypeStruct((2 * parts, rows, LANES), f32),
        compiler_params=pltpu.CompilerParams(vmem_limit_bytes=VMEM_LIMIT),
        name="prepare",
    )(tile)


def read_info(block, count):
    lane = lax.broadcasted_iota(jnp.int32, block.shape, 1)
    first = lax.broadcasted_iota(jnp.int32, block.shape, 0) == 0
    values = block.astype(f32)
    return [
        jnp.sum(jnp.where(first & (lane == j), values, 0.0)).astype(jnp.int32) for j in range(count)
    ]


def window(tile, plane, row, col, size, parts):
    shift = lax.rem(LANES - col, LANES)
    keep = lax.broadcasted_iota(jnp.int32, (size, LANES), 1) < LANES - col
    rolled = [
        pltpu.roll(tile[plane * parts + k, pl.ds(row, size), :], shift, 1) for k in range(size // LANES + 1)
    ]
    return jnp.concatenate(
        [jnp.where(keep, rolled[k], rolled[k + 1]) for k in range(size // LANES)], axis=1
    )


def side_by_side(stacked, size):
    return jnp.concatenate([stacked[:size], stacked[size:]], axis=1)


def terms_kernel(count, capacity, size, tile, probe, left, right, term_in, *rest):
    amps, outs, term, info = rest[:count], rest[count : 2 * count], rest[2 * count], rest[2 * count + 1]
    parts = tile.shape[0] // 2
    term[...] = term_in[...]
    for amp, out in zip(amps, outs):
        block = amp[pl.ds(capacity * size, INFO_ROWS), :]
        for j, number in enumerate(read_info(block, 3 * capacity)):
            info[j] = number

        def one(slot, carry, amp=amp, out=out):
            @pl.when(info[3 * slot + 2] > 0)
            def _():
                row = info[3 * slot]
                col = info[3 * slot + 1]
                patch_re = window(tile, 0, row, col, size, parts)
                patch_im = window(tile, 1, row, col, size, parts)
                probe_re = probe[0]
                probe_im = probe[1]
                psi_re = (probe_re * patch_re - probe_im * patch_im).astype(bf16)
                psi_im = (probe_re * patch_im + probe_im * patch_re).astype(bf16)
                half = dot(left[...], jnp.concatenate([psi_re, psi_im], axis=0)).astype(bf16)
                wave = dot(side_by_side(half, size), right[...])
                wave_re = wave[:, :size]
                wave_im = wave[:, size:]
                square = wave_re * wave_re + wave_im * wave_im
                measured = amp[pl.ds(pl.multiple_of(slot * size, size), size), :].astype(f32)
                factor = 1.0 - measured * lax.rsqrt(jnp.maximum(square, 0.25))
                diff_re = (wave_re * factor).astype(bf16)
                diff_im = (wave_im * factor).astype(bf16)
                back = dot(right[...], jnp.concatenate([diff_re, diff_im], axis=0)).astype(bf16)
                chi = dot(side_by_side(back, size), left[...])
                chi_re = chi[:, :size]
                chi_im = chi[:, size:]
                out[slot, 0] = (probe_re * chi_re + probe_im * chi_im).astype(bf16)
                out[slot, 1] = (probe_re * chi_im - probe_im * chi_re).astype(bf16)
                patch_re = window(tile, 0, row, col, size, parts)
                patch_im = window(tile, 1, row, col, size, parts)
                term[0] += patch_re * chi_re + patch_im * chi_im
                term[1] += patch_re * chi_im - patch_im * chi_re

            return carry

        lax.fori_loop(0, capacity, one, 0)


def terms(tile, probe, left, right, term, amps, capacity):
    size = probe.shape[1]
    count = len(amps)
    full = pl.BlockSpec(memory_space=pltpu.VMEM)
    work = 16 * 2 * size**3 * capacity * count
    results = pl.pallas_call(
        functools.partial(terms_kernel, count, capacity, size),
        in_specs=[full] * (5 + count),
        out_specs=[full] * (count + 1),
        out_shape=[jax.ShapeDtypeStruct((capacity, 2, size, size), bf16)] * count
        + [jax.ShapeDtypeStruct(term.shape, f32)],
        scratch_shapes=[pltpu.SMEM((3 * capacity,), jnp.int32)],
        compiler_params=pltpu.CompilerParams(vmem_limit_bytes=VMEM_LIMIT),
        cost_estimate=pl.CostEstimate(flops=4 * work, bytes_accessed=2**22, transcendentals=0),
        name="terms",
    )(tile, probe, left, right, term, *amps)
    return results[:count], results[count]


def scatter_kernel(count, capacity, size, base, *rest):
    amp_infos, grads, out, info = rest[:count], rest[count : 2 * count], rest[2 * count], rest[2 * count + 1]
    cols = base.shape[2]
    parts = cols // LANES
    acc = rest[2 * count + 2]
    for plane in range(2):
        for k in range(parts):
            acc[plane * parts + k] = base[plane, :, k * LANES : (k + 1) * LANES]
    inner = size // LANES
    for amp, grad in zip(amp_infos, grads):
        for j, number in enumerate(read_info(amp[...], 3 * capacity)):
            info[j] = number

        def one(slot, carry, grad=grad):
            @pl.when(info[3 * slot + 2] > 0)
            def _():
                row = info[3 * slot]
                col = info[3 * slot + 1]
                keep = lax.broadcasted_iota(jnp.int32, (size, LANES), 1) >= col
                zero = jnp.zeros((size, LANES), f32)
                for plane in range(2):
                    rolled = [
                        pltpu.roll(grad[slot, plane, :, k * LANES : (k + 1) * LANES].astype(f32), lax.rem(col, LANES), 1)
                        * 0.25
                        for k in range(inner)
                    ]
                    for k in range(inner + 1):
                        here = rolled[k] if k < inner else zero
                        before = rolled[k - 1] if k > 0 else zero
                        acc[plane * parts + k, pl.ds(row, size), :] -= jnp.where(keep, here, before)

            return carry

        lax.fori_loop(0, capacity, one, 0)
    for plane in range(2):
        for k in range(parts):
            out[plane, :, k * LANES : (k + 1) * LANES] = acc[plane * parts + k]


def scatter(base, infos, grads, capacity, size):
    count = len(grads)
    _, rows, cols = base.shape
    full = pl.BlockSpec(memory_space=pltpu.VMEM)
    return pl.pallas_call(
        functools.partial(scatter_kernel, count, capacity, size),
        in_specs=[full] * (1 + 2 * count),
        out_specs=full,
        out_shape=jax.ShapeDtypeStruct(base.shape, f32),
        scratch_shapes=[
            pltpu.SMEM((3 * capacity,), jnp.int32),
            pltpu.VMEM((2 * cols // LANES, rows, LANES), f32),
        ],
        compiler_params=pltpu.CompilerParams(vmem_limit_bytes=VMEM_LIMIT),
        cost_estimate=pl.CostEstimate(flops=2**30, bytes_accessed=2**23, transcendentals=0),
        name="scatter",
    )(base, *infos, *grads)


def with_halo(block, sides, width):
    for axis, dim in sides:
        count = lax.axis_size(axis)
        forward = [(i, (i + 1) % count) for i in range(count)]
        backward = [(target, source) for source, target in forward]
        low = lax.ppermute(lax.slice_in_dim(block, block.shape[dim] - width, None, axis=dim), axis, forward)
        high = lax.ppermute(lax.slice_in_dim(block, 0, width, axis=dim), axis, backward)
        block = jnp.concatenate([low, block, high], axis=dim)
    return block


def neighbours(tile):
    rows = with_halo(tile, (("obj", 1),), 1)
    cols = with_halo(tile, (("pos", 2),), 1)
    return rows[:, :-2] + rows[:, 2:] + cols[:, :, :-2] + cols[:, :, 2:]


def sum_everywhere(value):
    n_pos = lax.axis_size("pos")
    n_obj = lax.axis_size("obj")
    me = lax.axis_index("pos")
    rows = value.shape[1] // n_pos

    def piece(which):
        return lax.dynamic_slice_in_dim(value, which * rows, rows, axis=1)

    total = piece(me)
    for d in range(1, n_pos):
        total = total + exchange(piece(me ^ d), "pos", d)
    step = 1
    while step < n_obj:
        total = total + exchange(total, "obj", step)
        step *= 2
    result = lax.dynamic_update_slice_in_dim(value, total, me * rows, axis=1)
    for d in range(1, n_pos):
        result = lax.dynamic_update_slice_in_dim(result, exchange(total, "pos", d), (me ^ d) * rows, axis=1)
    return result


def shards(object_field, probe, amplitude, row_offset, col_offset, owner):
    n_pos = lax.axis_size("pos")
    n_obj = lax.axis_size("obj")
    pos_dev, size, _ = amplitude.shape
    capacity = max(2, pos_dev // n_pos + 1)
    left_np, right_np = dft_blocks(size)
    left = jnp.asarray(left_np)
    right = jnp.asarray(right_np)
    me = lax.axis_index("pos").astype(jnp.int32).reshape(1)
    packed = pack(me, owner, row_offset, col_offset, amplitude, n_pos, capacity)
    received = {0: packed[0]}
    order = [2, 4, 1, 3, 5, 6, 7] if n_pos == 8 else list(range(1, n_pos))
    for d in order:
        received[d] = exchange(packed[d], "pos", d)
    groups = [[0], [1], [2, 4], [3, 5], [6], [7]] if n_pos == 8 else [[d] for d in range(n_pos)]
    tile = prepare(object_field)
    term = jnp.zeros(probe.shape, f32)
    infos, grads = [], []
    for group in groups:
        outs, term = terms(tile, probe, left, right, term, [received[d] for d in group], capacity)
        grads += outs
        infos += [received[d][capacity * size :] for d in group]
    base = object_field - 0.125 * (4.0 * object_field - neighbours(object_field))
    new_object = scatter(base, infos, grads, capacity, size)
    probe_grad = sum_everywhere(term)
    new_probe = probe - probe_grad * (1.0 / math.sqrt(pos_dev * n_pos * n_obj))
    return (new_object, new_probe)


def solution(mesh):
    placed = (
        P(None, "obj", "pos"),
        P(),
        P(("pos", "obj"), None, None),
        P(("pos", "obj")),
        P(("pos", "obj")),
        P(("pos", "obj")),
    )
    return jax.shard_map(
        shards, mesh=mesh, in_specs=placed, out_specs=(P(None, "obj", "pos"), P()), check_vma=False
    )
```

```python
import functools
import math

import jax
import jax.numpy as jnp
import numpy as np
from jax import lax
from jax.experimental import pallas as pl
from jax.experimental.pallas import tpu as pltpu
from jax.sharding import PartitionSpec as P

LANES = 128
INFO_ROWS = 16
SUBLANES = 8
PACK_VMEM = 60 * 2**20
SMALL_VMEM = 16 * 2**20
TERMS_VMEM = 32 * 2**20
bf16 = jnp.bfloat16
f32 = jnp.float32


def dft_blocks(size):
    index = np.arange(size, dtype=np.int32)
    product = index[:, None] * index[None, :] % size
    angle = product.astype(np.float32) * np.float32(2.0 * math.pi / size)
    scale = np.float32(1.0 / math.sqrt(size))
    real_part = (np.cos(angle) * scale).astype(bf16)
    imag_part = (-np.sin(angle) * scale).astype(bf16)
    left = np.block([[real_part, -imag_part], [imag_part, real_part]])
    right = np.block([[real_part, imag_part], [-imag_part, real_part]])
    return left, right


def exchange(value, axis, distance):
    count = lax.axis_size(axis)
    return lax.ppermute(value, axis, [(i, i ^ distance) for i in range(count)])


def dot(a, b):
    return jnp.dot(a, b, preferred_element_type=f32)


def rim_width(cols, size):
    return -(-cols // size)


def pack_kernel(n_pos, capacity, order, owner_in, row_in, col_in, amp_in, tile, *rest):
    outs, rim = rest[:n_pos], rest[n_pos]
    owner, row, col, counts, source, amp, sides, ends, edges, info, rim_rows = rest[n_pos + 1 : n_pos + 12]
    int_sems, amp_sem, side_sems, end_sems, out_sems, info_sems = rest[n_pos + 12 :]
    pos_dev, size, _ = amp_in.shape
    _, rows, cols = tile.shape
    int_loads = [
        pltpu.make_async_copy(src, dst, int_sems.at[i])
        for i, (src, dst) in enumerate(((owner_in, owner), (row_in, row), (col_in, col)))
    ]
    amp_load = pltpu.make_async_copy(amp_in, amp, amp_sem)
    side_loads = [
        pltpu.make_async_copy(tile.at[:, :, pl.ds(first, LANES)], sides.at[i], side_sems.at[i])
        for i, first in enumerate((0, cols - LANES))
    ]
    end_loads = [
        pltpu.make_async_copy(tile.at[:, pl.ds(first, SUBLANES), :], ends.at[i], end_sems.at[i])
        for i, first in enumerate((0, rows - SUBLANES))
    ]
    for load in int_loads + [amp_load] + end_loads + side_loads:
        load.start()
    me = lax.axis_index("pos")
    for slot in range(n_pos * capacity):
        source[slot] = 0
    for q in range(n_pos):
        counts[q] = 0
    for load in int_loads:
        load.wait()
    for item in range(pos_dev):
        who = owner[item]
        rank = counts[who]
        source[who * capacity + rank] = item
        counts[who] = rank + 1
    stores = []
    amp_load.wait()
    for d in order:
        partner = jnp.bitwise_xor(me, d)
        for k in range(capacity):
            item = source[partner * capacity + k]
            store = pltpu.make_async_copy(amp.at[item], outs[d].at[pl.ds(k * size, size)], out_sems.at[d, k])
            store.start()
            stores.append(store)
    edges[...] = jnp.zeros(edges.shape, f32)
    place = 1
    for i, lane_of_edge in enumerate((0, LANES - 1)):
        pick = (lax.broadcasted_iota(jnp.int32, (SUBLANES, LANES), 1) == lane_of_edge).astype(bf16)
        side_loads[i].wait()
        for plane in range(2):
            turned = lax.dot_general(
                pick, sides[i, plane].astype(bf16), (((1,), (1,)), ((), ())), preferred_element_type=f32
            )
            for part in range(rows // size):
                edges[place : place + 1, :] = turned[0:1, part * size : (part + 1) * size]
                place += 1
    edge_block = edges[...]
    lane = lax.broadcasted_iota(jnp.int32, (INFO_ROWS, size), 1)
    at_info = lax.broadcasted_iota(jnp.int32, (INFO_ROWS, size), 0) == 0
    for d in order:
        partner = jnp.bitwise_xor(me, d)
        held = counts[partner]
        block = jnp.zeros((INFO_ROWS, size), f32)
        for k in range(capacity):
            item = source[partner * capacity + k]
            for j, number in enumerate((row[item], col[item], (k < held).astype(jnp.int32))):
                block = jnp.where(lane == 3 * k + j, number.astype(f32), block)
        info[d] = jnp.where(at_info, block, edge_block).astype(bf16)
        store = pltpu.make_async_copy(info.at[d], outs[d].at[pl.ds(capacity * size, INFO_ROWS)], info_sems.at[d])
        store.start()
        stores.append(store)
    rim_rows[...] = jnp.zeros(rim_rows.shape, f32)
    for i, at in enumerate((0, SUBLANES - 1)):
        end_loads[i].wait()
        for plane in range(2):
            for part, first in enumerate(range(0, cols, size)):
                width = min(size, cols - first)
                place = i * rim_width(cols, size) + part
                rim_rows[plane, place : place + 1, :width] = ends[i, plane, at : at + 1, first : first + width]
    store = pltpu.make_async_copy(rim_rows, rim, end_sems.at[2])
    store.start()
    stores.append(store)
    for store in stores:
        store.wait()


def pack(owner, row, col, amplitude, tile, n_pos, capacity, order):
    pos_dev, size, _ = amplitude.shape
    _, rows, cols = tile.shape
    far = pl.BlockSpec(memory_space=pltpu.HBM)
    ints = pltpu.SMEM((pos_dev,), jnp.int32)
    return pl.pallas_call(
        functools.partial(pack_kernel, n_pos, capacity, order),
        in_specs=[far] * 5,
        out_specs=[far] * (n_pos + 1),
        out_shape=[jax.ShapeDtypeStruct((capacity * size + INFO_ROWS, size), bf16)] * n_pos
        + [jax.ShapeDtypeStruct((2, SUBLANES, size), f32)],
        scratch_shapes=[
            ints,
            ints,
            ints,
            pltpu.SMEM((n_pos,), jnp.int32),
            pltpu.SMEM((n_pos * capacity,), jnp.int32),
            pltpu.VMEM(amplitude.shape, bf16),
            pltpu.VMEM((2, 2, rows, LANES), f32),
            pltpu.VMEM((2, 2, SUBLANES, cols), f32),
            pltpu.VMEM((INFO_ROWS, size), f32),
            pltpu.VMEM((n_pos, INFO_ROWS, size), bf16),
            pltpu.VMEM((2, SUBLANES, size), f32),
            pltpu.SemaphoreType.DMA((3,)),
            pltpu.SemaphoreType.DMA,
            pltpu.SemaphoreType.DMA((2,)),
            pltpu.SemaphoreType.DMA((3,)),
            pltpu.SemaphoreType.DMA((n_pos, capacity)),
            pltpu.SemaphoreType.DMA((n_pos,)),
        ],
        compiler_params=pltpu.CompilerParams(vmem_limit_bytes=PACK_VMEM),
        cost_estimate=pl.CostEstimate(flops=2**20, bytes_accessed=2**20, transcendentals=0),
        name="pack",
    )(owner, row, col, amplitude, tile)


def read_info(block, count):
    lane = lax.broadcasted_iota(jnp.int32, block.shape, 1)
    first = lax.broadcasted_iota(jnp.int32, block.shape, 0) == 0
    values = block.astype(f32)
    return [jnp.sum(jnp.where(first & (lane == j), values, 0.0)).astype(jnp.int32) for j in range(count)]


def window(tile, plane, row, col, size, parts):
    shift = lax.rem(LANES - col, LANES)
    keep = lax.broadcasted_iota(jnp.int32, (size, LANES), 1) < LANES - col
    rolled = [pltpu.roll(tile[plane * parts + k, pl.ds(row, size), :], shift, 1) for k in range(size // LANES + 1)]
    return jnp.concatenate([jnp.where(keep, rolled[k], rolled[k + 1]) for k in range(size // LANES)], axis=1)


def add_window(acc, plane, row, col, value, size, parts):
    inner = size // LANES
    keep = lax.broadcasted_iota(jnp.int32, (size, LANES), 1) >= col
    zero = jnp.zeros((size, LANES), f32)
    rolled = [pltpu.roll(value[:, k * LANES : (k + 1) * LANES], lax.rem(col, LANES), 1) for k in range(inner)]
    for k in range(inner + 1):
        here = rolled[k] if k < inner else zero
        before = rolled[k - 1] if k > 0 else zero
        acc[plane * parts + k, pl.ds(row, size), :] += jnp.where(keep, here, before)


def side_by_side(stacked, size):
    return jnp.concatenate([stacked[:size], stacked[size:]], axis=1)


def buffer_terms(amp, amp_load, info, tile, probe, left, right, acc, term, capacity, size, parts):
    numbers = read_info(info, 3 * capacity)
    slots = [tuple(numbers[3 * k : 3 * k + 3]) for k in range(capacity)]
    probe_re = probe[0]
    probe_im = probe[1]
    patches, psis = [], []
    for row, col, _ in slots:
        patch_re = window(tile, 0, row, col, size, parts)
        patch_im = window(tile, 1, row, col, size, parts)
        patches.append((patch_re.astype(bf16), patch_im.astype(bf16)))
        psi_re = (probe_re * patch_re - probe_im * patch_im).astype(bf16)
        psi_im = (probe_re * patch_im + probe_im * patch_re).astype(bf16)
        psis.append(jnp.concatenate([psi_re, psi_im], axis=0))
    halves = [side_by_side(dot(left[...], psi).astype(bf16), size) for psi in psis]
    waves = [dot(half, right[...]) for half in halves]
    diffs = []
    amp_load.wait()
    for k, wave in enumerate(waves):
        wave_re = wave[:, :size]
        wave_im = wave[:, size:]
        square = wave_re * wave_re + wave_im * wave_im
        measured = amp[k * size : (k + 1) * size, :].astype(f32)
        factor = 1.0 - measured * lax.rsqrt(jnp.maximum(square, 0.25))
        diffs.append(jnp.concatenate([(wave_re * factor).astype(bf16), (wave_im * factor).astype(bf16)], axis=0))
    backs = [side_by_side(dot(right[...], diff).astype(bf16), size) for diff in diffs]
    chis = [dot(back, left[...]) for back in backs]
    sum_re = sum_im = 0.0
    for (row, col, valid), (patch_re, patch_im), chi in zip(slots, patches, chis):
        weight = valid.astype(f32)
        chi_re = chi[:, :size] * weight
        chi_im = chi[:, size:] * weight
        grad_re = (probe_re * chi_re + probe_im * chi_im).astype(bf16).astype(f32)
        grad_im = (probe_re * chi_im - probe_im * chi_re).astype(bf16).astype(f32)
        add_window(acc, 0, row, col, grad_re, size, parts)
        add_window(acc, 1, row, col, grad_im, size, parts)
        patch_re = patch_re.astype(f32)
        patch_im = patch_im.astype(f32)
        sum_re += patch_re * chi_re + patch_im * chi_im
        sum_im += patch_re * chi_im - patch_im * chi_re
    term[0] += sum_re
    term[1] += sum_im


def terms_kernel(count, capacity, first, last, probe, left, right, *rest):
    size = probe.shape[1]
    held, infos, sems = rest[-3:]
    messages, rest = rest[:count], rest[count:-3]
    info_loads, amp_loads = [], []
    for i, message in enumerate(messages):
        info_rows = pl.ds(capacity * size, INFO_ROWS)
        amp_rows = pl.ds(0, capacity * size)
        info_loads.append(pltpu.make_async_copy(message.at[info_rows], infos.at[i], sems.at[i, 0]))
        amp_loads.append(pltpu.make_async_copy(message.at[amp_rows], held.at[i], sems.at[i, 1]))
    for load in info_loads + amp_loads:
        load.start()
    if first:
        source, tile, acc, term = rest
        parts = tile.shape[0] // 2
        for plane in range(2):
            for k in range(parts):
                block = source[plane, :, k * LANES : (k + 1) * LANES]
                tile[plane * parts + k] = block.astype(bf16).astype(f32)
        acc[...] = jnp.zeros(acc.shape, f32)
        term[...] = jnp.zeros(term.shape, f32)
    else:
        tile, acc_in, term_in, acc = rest[:4]
        term = rest[-1]
        parts = tile.shape[0] // 2
        acc[...] = acc_in[...]
        term[...] = term_in[...]
    for i in range(count):
        info_loads[i].wait()
        buffer_terms(
            held.at[i], amp_loads[i], infos[i], tile, probe, left, right, acc, term, capacity, size, parts
        )
    if last:
        keep, send = rest[4:6]
        half = size // 2
        odd = lax.rem(lax.axis_index("pos"), 2)
        keep[...] = term[:, pl.ds(pl.multiple_of(odd * half, half), half), :]
        send[...] = term[:, pl.ds(pl.multiple_of((1 - odd) * half, half), half), :]


def terms(probe, left, right, messages, capacity, source=None, state=None, last=False):
    size = probe.shape[1]
    count = len(messages)
    full = pl.BlockSpec(memory_space=pltpu.VMEM)
    far = pl.BlockSpec(memory_space=pltpu.HBM)
    scratch = [
        pltpu.VMEM((count, capacity * size, size), bf16),
        pltpu.VMEM((count, INFO_ROWS, size), bf16),
        pltpu.SemaphoreType.DMA((count, 2)),
    ]
    if state is None:
        _, rows, cols = source.shape
        blocks = jax.ShapeDtypeStruct((2 * cols // LANES, rows, LANES), f32)
        operands = (source,)
        shapes = [blocks, blocks, jax.ShapeDtypeStruct(probe.shape, f32)]
        aliases = {}
    else:
        operands = state
        tile, acc, term = state
        shapes = [jax.ShapeDtypeStruct(acc.shape, f32)]
        aliases = {4 + count: 0}
        if last:
            shapes += [jax.ShapeDtypeStruct((2, size // 2, size), f32)] * 2
            scratch = [pltpu.VMEM(term.shape, f32)] + scratch
        else:
            shapes += [jax.ShapeDtypeStruct(term.shape, f32)]
            aliases[5 + count] = 1
    results = pl.pallas_call(
        functools.partial(terms_kernel, count, capacity, state is None, last),
        in_specs=[full] * 3 + [far] * count + [full] * len(operands),
        out_specs=[full] * len(shapes),
        out_shape=shapes,
        scratch_shapes=scratch,
        input_output_aliases=aliases,
        compiler_params=pltpu.CompilerParams(vmem_limit_bytes=TERMS_VMEM),
        cost_estimate=pl.CostEstimate(
            flops=2 * size**3 * capacity * count, bytes_accessed=2**18, transcendentals=0
        ),
        name="terms",
    )(probe, left, right, *messages, *operands)
    return tuple(results) if state is None or last else (state[0], *results)


def finish_kernel(n_pos, n_obj, ring, steps, capacity, size, tile, acc, *rest):
    ends, rest = rest[: len(steps)], rest[len(steps) :]
    messages, (out, infos, chosen, sems) = rest[: len(ring)], rest[len(ring) :]
    loads = [
        pltpu.make_async_copy(message.at[pl.ds(capacity * size, INFO_ROWS)], infos.at[i], sems.at[i])
        for i, message in enumerate(messages)
    ]
    for load in loads:
        load.start()
    for load in loads:
        load.wait()
    _, rows, cols = tile.shape
    parts = cols // LANES
    each = rows // size
    me = lax.axis_index("pos")
    for side, neighbour in enumerate((lax.rem(me + n_pos - 1, n_pos), lax.rem(me + 1, n_pos))):
        block = jnp.zeros((INFO_ROWS, size), f32)
        for i, d in enumerate(ring):
            block = jnp.where(jnp.bitwise_xor(me, neighbour) == d, infos[i].astype(f32), block)
        chosen[side] = block

    def edge(side, plane):
        place = 1 + (2 * each if side == 0 else 0) + plane * each
        values = [chosen[side, place + i : place + i + 1, :] for i in range(each)]
        return jnp.concatenate([jnp.transpose(jnp.broadcast_to(v, (LANES, size))) for v in values], axis=0)

    level = lax.axis_index("obj")
    rim_at = ends[0].shape[1] - SUBLANES

    def end_row(side, plane, k):
        neighbour = lax.rem(level + (n_obj - 1 if side == 0 else 1), n_obj)
        place = rim_at + (rim_width(cols, size) if side == 0 else 0) + k * LANES // size
        lanes = slice(k * LANES % size, k * LANES % size + LANES)
        value = jnp.zeros((1, LANES), f32)
        for block, step in zip(ends, steps):
            value = jnp.where(jnp.bitwise_xor(level, neighbour) == step, block[plane, place : place + 1, lanes], value)
        return value

    lane = lax.broadcasted_iota(jnp.int32, (rows, LANES), 1)
    line = lax.broadcasted_iota(jnp.int32, (rows, LANES), 0)
    for plane in range(2):
        blocks = [tile[plane, :, k * LANES : (k + 1) * LANES] for k in range(parts)]
        to_right = [pltpu.roll(block, 1, 1) for block in blocks]
        to_left = [pltpu.roll(block, LANES - 1, 1) for block in blocks]
        low, high = edge(0, plane), edge(1, plane)
        for k in range(parts):
            here = slice(k * LANES, (k + 1) * LANES)
            block = blocks[k]
            near = jnp.where(lane == 0, to_right[k - 1] if k > 0 else low, to_right[k])
            near += jnp.where(lane == LANES - 1, to_left[k + 1] if k + 1 < parts else high, to_left[k])
            near += jnp.where(line == 0, end_row(0, plane, k), pltpu.roll(block, 1, 0))
            near += jnp.where(line == rows - 1, end_row(1, plane, k), pltpu.roll(block, rows - 1, 0))
            smooth = 4.0 * block - near
            out[plane, :, here] = block - 0.25 * (acc[plane * parts + k] + 0.5 * smooth)


def finish(tile, acc, steps, ends, ring, messages, n_pos, n_obj, capacity, size):
    full = pl.BlockSpec(memory_space=pltpu.VMEM)
    far = pl.BlockSpec(memory_space=pltpu.HBM)
    return pl.pallas_call(
        functools.partial(finish_kernel, n_pos, n_obj, ring, steps, capacity, size),
        in_specs=[full] * (2 + len(ends)) + [far] * len(ring),
        out_specs=full,
        out_shape=jax.ShapeDtypeStruct(tile.shape, f32),
        scratch_shapes=[
            pltpu.VMEM((len(ring), INFO_ROWS, size), bf16),
            pltpu.VMEM((2, INFO_ROWS, size), f32),
            pltpu.SemaphoreType.DMA((len(ring),)),
        ],
        compiler_params=pltpu.CompilerParams(vmem_limit_bytes=SMALL_VMEM),
        cost_estimate=pl.CostEstimate(flops=2**24, bytes_accessed=2**23, transcendentals=0),
        name="finish",
    )(tile, acc, *ends, *messages)


def small_call(body, name, operands, shapes):
    return pl.pallas_call(
        body,
        out_shape=shapes,
        compiler_params=pltpu.CompilerParams(vmem_limit_bytes=SMALL_VMEM),
        name=name,
    )(*operands)


def split_kernel(pairs, keep, got, *pieces):
    rows = pieces[0].shape[1]
    pair = lax.axis_index("pos") // 2
    for d in range(pairs):
        here = pl.ds(pl.multiple_of(jnp.bitwise_xor(pair, d) * rows, rows), rows)
        pieces[d][...] = keep[:, here, :] + got[:, here, :]


def join_kernel(pairs, scale, probe, *rest):
    pieces, out = rest[:pairs], rest[pairs]
    rows = pieces[0].shape[1]
    half = out.shape[1]
    me = lax.axis_index("pos")
    for d in range(pairs):
        start = jnp.bitwise_xor(me // 2, d) * rows
        old = probe[:, pl.ds(pl.multiple_of(lax.rem(me, 2) * half + start, rows), rows), :]
        out[:, pl.ds(pl.multiple_of(start, rows), rows), :] = old - pieces[d][...] * scale


def whole_kernel(mine, other, out):
    half = mine.shape[1]
    odd = lax.rem(lax.axis_index("pos"), 2)
    out[:, pl.ds(pl.multiple_of(odd * half, half), half), :] = mine[...]
    out[:, pl.ds(pl.multiple_of((1 - odd) * half, half), half), :] = other[...]


def step_probe(probe, keep, send, scale, rim, beside):
    n_pos = lax.axis_size("pos")
    n_obj = lax.axis_size("obj")
    pairs = n_pos // 2
    planes, half, size = keep.shape
    rows = half // pairs
    shape = jax.ShapeDtypeStruct((planes, rows, size), f32)
    got = exchange(send, "pos", 1)
    pieces = small_call(functools.partial(split_kernel, pairs), "split", (keep, got), [shape] * pairs)
    total = pieces[0]
    for d in range(1, pairs):
        total = total + exchange(pieces[d], "pos", 2 * d)
    steps, ends = [], []
    while 2 ** len(steps) < n_obj:
        step = 2 ** (len(steps) + 1) - 1
        got = exchange(jnp.concatenate([total, rim], axis=1), "obj", step)
        total = total + got[:, :rows]
        steps.append(step)
        ends.append(got)
    gathered = [total] + [exchange(total, "pos", 2 * d) for d in range(1, pairs)]
    gathered, result = lax.optimization_barrier((gathered, beside(steps, ends)))
    mine = small_call(
        functools.partial(join_kernel, pairs, scale),
        "join",
        (probe, *gathered),
        jax.ShapeDtypeStruct(keep.shape, f32),
    )
    other = exchange(mine, "pos", 1)
    new_probe = small_call(whole_kernel, "whole", (mine, other), jax.ShapeDtypeStruct(probe.shape, f32))
    return new_probe, result


def shards(object_field, probe, amplitude, row_offset, col_offset, owner):
    n_pos = lax.axis_size("pos")
    n_obj = lax.axis_size("obj")
    pos_dev, size, _ = amplitude.shape
    capacity = max(2, pos_dev // n_pos + 1)
    left, right = (jnp.asarray(table) for table in dft_blocks(size))
    if n_pos == 8:
        early, later = [1, 2, 4, 3, 5], {4: [6], 3: [7]}
        order = [0, 1, 2, 4, 3, 5, 6, 7]
    else:
        window = 4
        order = list(range(n_pos))
        early, later = order[1 : 1 + window], {d: [d + window] for d in order[1 : n_pos - window]}
    *packed, rim = pack(
        owner, row_offset, col_offset, amplitude, object_field, n_pos, capacity, order[1:] + order[:1]
    )
    received = {d: exchange(packed[d], "pos", d) for d in early}
    received[0] = packed[0]
    state = terms(probe, left, right, [received[0]], capacity, source=object_field)
    for d in order[1:-1]:
        state = terms(probe, left, right, [received[d]], capacity, state=state)
        for e in later.get(d, []):
            state, sending = lax.optimization_barrier((state, packed[e]))
            received[e] = exchange(sending, "pos", e)
    acc, keep, send = terms(probe, left, right, [received[order[-1]]], capacity, state=state, last=True)
    ring = sorted({i ^ ((i + 1) % n_pos) for i in range(n_pos)})
    near = [received[d] for d in ring]

    def object_step(steps, ends):
        return finish(object_field, acc, steps, ends, ring, near, n_pos, n_obj, capacity, size)

    scale = 1.0 / math.sqrt(pos_dev * n_pos * n_obj)
    new_probe, new_object = step_probe(probe, keep, send, scale, rim, object_step)
    return (new_object, new_probe)


def solution(mesh):
    placed = (
        P(None, "obj", "pos"),
        P(),
        P(("pos", "obj"), None, None),
        P(("pos", "obj")),
        P(("pos", "obj")),
        P(("pos", "obj")),
    )
    return jax.shard_map(
        shards, mesh=mesh, in_specs=placed, out_specs=(P(None, "obj", "pos"), P()), check_vma=False
    )
```

```python
import functools
import math

import jax
import jax.numpy as jnp
import numpy as np
from jax import lax
from jax.experimental import pallas as pl
from jax.experimental.pallas import tpu as pltpu
from jax.sharding import PartitionSpec as P

LANES = 128
INFO_ROWS = 16
SUBLANES = 8
PACK_VMEM = 60 * 2**20
SMALL_VMEM = 16 * 2**20
TERMS_VMEM = 32 * 2**20
bf16 = jnp.bfloat16
f32 = jnp.float32


def dft_blocks(size):
    index = np.arange(size, dtype=np.int32)
    product = index[:, None] * index[None, :] % size
    angle = product.astype(np.float32) * np.float32(2.0 * math.pi / size)
    scale = np.float32(1.0 / math.sqrt(size))
    real_part = (np.cos(angle) * scale).astype(bf16)
    imag_part = (-np.sin(angle) * scale).astype(bf16)
    left = np.block([[real_part, -imag_part], [imag_part, real_part]])
    right = np.block([[real_part, imag_part], [-imag_part, real_part]])
    return left, right


def exchange(value, axis, distance):
    count = lax.axis_size(axis)
    return lax.ppermute(value, axis, [(i, i ^ distance) for i in range(count)])


def dot(a, b):
    return jnp.dot(a, b, preferred_element_type=f32)


def rim_width(cols, size):
    return -(-cols // size)


def pack_kernel(n_pos, capacity, order, owner_in, row_in, col_in, amp_in, tile, *rest):
    outs, rim = rest[:n_pos], rest[n_pos]
    owner, row, col, counts, source, amp, sides, ends, edges, info, rim_rows = rest[n_pos + 1 : n_pos + 12]
    int_sems, amp_sem, side_sems, end_sems, out_sems, info_sems = rest[n_pos + 12 :]
    pos_dev, size, _ = amp_in.shape
    _, rows, cols = tile.shape
    int_loads = [
        pltpu.make_async_copy(src, dst, int_sems.at[i])
        for i, (src, dst) in enumerate(((owner_in, owner), (row_in, row), (col_in, col)))
    ]
    amp_load = pltpu.make_async_copy(amp_in, amp, amp_sem)
    side_loads = [
        pltpu.make_async_copy(tile.at[:, :, pl.ds(first, LANES)], sides.at[i], side_sems.at[i])
        for i, first in enumerate((0, cols - LANES))
    ]
    end_loads = [
        pltpu.make_async_copy(tile.at[:, pl.ds(first, SUBLANES), :], ends.at[i], end_sems.at[i])
        for i, first in enumerate((0, rows - SUBLANES))
    ]
    for load in int_loads + [amp_load] + end_loads + side_loads:
        load.start()
    me = lax.axis_index("pos")
    for slot in range(n_pos * capacity):
        source[slot] = 0
    for q in range(n_pos):
        counts[q] = 0
    for load in int_loads:
        load.wait()
    for item in range(pos_dev):
        who = owner[item]
        rank = counts[who]
        source[who * capacity + rank] = item
        counts[who] = rank + 1
    stores = []
    amp_load.wait()
    for d in order:
        partner = jnp.bitwise_xor(me, d)
        for k in range(capacity):
            item = source[partner * capacity + k]
            store = pltpu.make_async_copy(amp.at[item], outs[d].at[pl.ds(k * size, size)], out_sems.at[d, k])
            store.start()
            stores.append(store)
    edges[...] = jnp.zeros(edges.shape, f32)
    place = 1
    for i, lane_of_edge in enumerate((0, LANES - 1)):
        pick = (lax.broadcasted_iota(jnp.int32, (SUBLANES, LANES), 1) == lane_of_edge).astype(bf16)
        side_loads[i].wait()
        for plane in range(2):
            turned = lax.dot_general(
                pick, sides[i, plane].astype(bf16), (((1,), (1,)), ((), ())), preferred_element_type=f32
            )
            for part in range(rows // size):
                edges[place : place + 1, :] = turned[0:1, part * size : (part + 1) * size]
                place += 1
    edge_block = edges[...]
    lane = lax.broadcasted_iota(jnp.int32, (INFO_ROWS, size), 1)
    at_info = lax.broadcasted_iota(jnp.int32, (INFO_ROWS, size), 0) == 0
    for d in order:
        partner = jnp.bitwise_xor(me, d)
        held = counts[partner]
        block = jnp.zeros((INFO_ROWS, size), f32)
        for k in range(capacity):
            item = source[partner * capacity + k]
            for j, number in enumerate((row[item], col[item], (k < held).astype(jnp.int32))):
                block = jnp.where(lane == 3 * k + j, number.astype(f32), block)
        info[d] = jnp.where(at_info, block, edge_block).astype(bf16)
        store = pltpu.make_async_copy(info.at[d], outs[d].at[pl.ds(capacity * size, INFO_ROWS)], info_sems.at[d])
        store.start()
        stores.append(store)
    rim_rows[...] = jnp.zeros(rim_rows.shape, f32)
    for i, at in enumerate((0, SUBLANES - 1)):
        end_loads[i].wait()
        for plane in range(2):
            for part, first in enumerate(range(0, cols, size)):
                width = min(size, cols - first)
                place = i * rim_width(cols, size) + part
                rim_rows[plane, place : place + 1, :width] = ends[i, plane, at : at + 1, first : first + width]
    store = pltpu.make_async_copy(rim_rows, rim, end_sems.at[2])
    store.start()
    stores.append(store)
    for store in stores:
        store.wait()


def pack(owner, row, col, amplitude, tile, n_pos, capacity, order):
    pos_dev, size, _ = amplitude.shape
    _, rows, cols = tile.shape
    far = pl.BlockSpec(memory_space=pltpu.HBM)
    ints = pltpu.SMEM((pos_dev,), jnp.int32)
    return pl.pallas_call(
        functools.partial(pack_kernel, n_pos, capacity, order),
        in_specs=[far] * 5,
        out_specs=[far] * (n_pos + 1),
        out_shape=[jax.ShapeDtypeStruct((capacity * size + INFO_ROWS, size), bf16)] * n_pos
        + [jax.ShapeDtypeStruct((2, SUBLANES, size), f32)],
        scratch_shapes=[
            ints,
            ints,
            ints,
            pltpu.SMEM((n_pos,), jnp.int32),
            pltpu.SMEM((n_pos * capacity,), jnp.int32),
            pltpu.VMEM(amplitude.shape, bf16),
            pltpu.VMEM((2, 2, rows, LANES), f32),
            pltpu.VMEM((2, 2, SUBLANES, cols), f32),
            pltpu.VMEM((INFO_ROWS, size), f32),
            pltpu.VMEM((n_pos, INFO_ROWS, size), bf16),
            pltpu.VMEM((2, SUBLANES, size), f32),
            pltpu.SemaphoreType.DMA((3,)),
            pltpu.SemaphoreType.DMA,
            pltpu.SemaphoreType.DMA((2,)),
            pltpu.SemaphoreType.DMA((3,)),
            pltpu.SemaphoreType.DMA((n_pos, capacity)),
            pltpu.SemaphoreType.DMA((n_pos,)),
        ],
        compiler_params=pltpu.CompilerParams(vmem_limit_bytes=PACK_VMEM),
        cost_estimate=pl.CostEstimate(flops=2**20, bytes_accessed=2**20, transcendentals=0),
        name="pack",
    )(owner, row, col, amplitude, tile)


def read_info(block, count):
    lane = lax.broadcasted_iota(jnp.int32, block.shape, 1)
    first = lax.broadcasted_iota(jnp.int32, block.shape, 0) == 0
    values = block.astype(f32)
    return [jnp.sum(jnp.where(first & (lane == j), values, 0.0)).astype(jnp.int32) for j in range(count)]


def window(tile, plane, row, col, size, parts):
    shift = lax.rem(LANES - col, LANES)
    keep = lax.broadcasted_iota(jnp.int32, (size, LANES), 1) < LANES - col
    rolled = [pltpu.roll(tile[plane * parts + k, pl.ds(row, size), :], shift, 1) for k in range(size // LANES + 1)]
    return jnp.concatenate([jnp.where(keep, rolled[k], rolled[k + 1]) for k in range(size // LANES)], axis=1)


def add_window(acc, plane, row, col, value, size, parts):
    inner = size // LANES
    keep = lax.broadcasted_iota(jnp.int32, (size, LANES), 1) >= col
    zero = jnp.zeros((size, LANES), f32)
    rolled = [pltpu.roll(value[:, k * LANES : (k + 1) * LANES], lax.rem(col, LANES), 1) for k in range(inner)]
    for k in range(inner + 1):
        here = rolled[k] if k < inner else zero
        before = rolled[k - 1] if k > 0 else zero
        acc[plane * parts + k, pl.ds(row, size), :] += jnp.where(keep, here, before)


def side_by_side(stacked, size):
    return jnp.concatenate([stacked[:size], stacked[size:]], axis=1)


def buffer_terms(amp, amp_load, info, tile, probe, left, right, acc, term, capacity, size, parts):
    numbers = read_info(info, 3 * capacity)
    slots = [tuple(numbers[3 * k : 3 * k + 3]) for k in range(capacity)]
    probe_re = probe[0]
    probe_im = probe[1]
    patches, psis = [], []
    for row, col, _ in slots:
        patch_re = window(tile, 0, row, col, size, parts)
        patch_im = window(tile, 1, row, col, size, parts)
        patches.append((patch_re.astype(bf16), patch_im.astype(bf16)))
        psi_re = (probe_re * patch_re - probe_im * patch_im).astype(bf16)
        psi_im = (probe_re * patch_im + probe_im * patch_re).astype(bf16)
        psis.append(jnp.concatenate([psi_re, psi_im], axis=0))
    halves = [side_by_side(dot(left[...], psi).astype(bf16), size) for psi in psis]
    waves = [dot(half, right[...]) for half in halves]
    diffs = []
    amp_load.wait()
    for k, wave in enumerate(waves):
        wave_re = wave[:, :size]
        wave_im = wave[:, size:]
        square = wave_re * wave_re + wave_im * wave_im
        measured = amp[k * size : (k + 1) * size, :].astype(f32)
        factor = 1.0 - measured * lax.rsqrt(jnp.maximum(square, 0.25))
        diffs.append(jnp.concatenate([(wave_re * factor).astype(bf16), (wave_im * factor).astype(bf16)], axis=0))
    backs = [side_by_side(dot(right[...], diff).astype(bf16), size) for diff in diffs]
    chis = [dot(back, left[...]) for back in backs]
    sum_re = sum_im = 0.0
    for (row, col, valid), (patch_re, patch_im), chi in zip(slots, patches, chis):
        weight = valid.astype(f32)
        chi_re = chi[:, :size] * weight
        chi_im = chi[:, size:] * weight
        grad_re = (probe_re * chi_re + probe_im * chi_im).astype(bf16).astype(f32)
        grad_im = (probe_re * chi_im - probe_im * chi_re).astype(bf16).astype(f32)
        add_window(acc, 0, row, col, grad_re, size, parts)
        add_window(acc, 1, row, col, grad_im, size, parts)
        patch_re = patch_re.astype(f32)
        patch_im = patch_im.astype(f32)
        sum_re += patch_re * chi_re + patch_im * chi_im
        sum_im += patch_re * chi_im - patch_im * chi_re
    term[0] += sum_re
    term[1] += sum_im


def terms_kernel(count, capacity, first, last, probe, left, right, *rest):
    size = probe.shape[1]
    held, infos, sems = rest[-3:]
    messages, rest = rest[:count], rest[count:-3]
    info_loads, amp_loads = [], []
    for i, message in enumerate(messages):
        info_rows = pl.ds(capacity * size, INFO_ROWS)
        amp_rows = pl.ds(0, capacity * size)
        info_loads.append(pltpu.make_async_copy(message.at[info_rows], infos.at[i], sems.at[i, 0]))
        amp_loads.append(pltpu.make_async_copy(message.at[amp_rows], held.at[i], sems.at[i, 1]))
    for load in info_loads + amp_loads:
        load.start()
    if first:
        source, tile, acc, term = rest
        parts = tile.shape[0] // 2
        for plane in range(2):
            for k in range(parts):
                block = source[plane, :, k * LANES : (k + 1) * LANES]
                tile[plane * parts + k] = block.astype(bf16).astype(f32)
        acc[...] = jnp.zeros(acc.shape, f32)
        term[...] = jnp.zeros(term.shape, f32)
    else:
        tile, acc_in, term_in, acc = rest[:4]
        term = rest[-1]
        parts = tile.shape[0] // 2
        acc[...] = acc_in[...]
        term[...] = term_in[...]
    for i in range(count):
        info_loads[i].wait()
        buffer_terms(
            held.at[i], amp_loads[i], infos[i], tile, probe, left, right, acc, term, capacity, size, parts
        )
    if last:
        keep, send = rest[4:6]
        half = size // 2
        odd = lax.rem(lax.axis_index("pos"), 2)
        keep[...] = term[:, pl.ds(pl.multiple_of(odd * half, half), half), :]
        send[...] = term[:, pl.ds(pl.multiple_of((1 - odd) * half, half), half), :]


def terms(probe, left, right, messages, capacity, source=None, state=None, last=False):
    size = probe.shape[1]
    count = len(messages)
    full = pl.BlockSpec(memory_space=pltpu.VMEM)
    far = pl.BlockSpec(memory_space=pltpu.HBM)
    scratch = [
        pltpu.VMEM((count, capacity * size, size), bf16),
        pltpu.VMEM((count, INFO_ROWS, size), bf16),
        pltpu.SemaphoreType.DMA((count, 2)),
    ]
    if state is None:
        _, rows, cols = source.shape
        blocks = jax.ShapeDtypeStruct((2 * cols // LANES, rows, LANES), f32)
        operands = (source,)
        shapes = [blocks, blocks, jax.ShapeDtypeStruct(probe.shape, f32)]
        aliases = {}
    else:
        operands = state
        tile, acc, term = state
        shapes = [jax.ShapeDtypeStruct(acc.shape, f32)]
        aliases = {4 + count: 0}
        if last:
            shapes += [jax.ShapeDtypeStruct((2, size // 2, size), f32)] * 2
            scratch = [pltpu.VMEM(term.shape, f32)] + scratch
        else:
            shapes += [jax.ShapeDtypeStruct(term.shape, f32)]
            aliases[5 + count] = 1
    results = pl.pallas_call(
        functools.partial(terms_kernel, count, capacity, state is None, last),
        in_specs=[full] * 3 + [far] * count + [full] * len(operands),
        out_specs=[full] * len(shapes),
        out_shape=shapes,
        scratch_shapes=scratch,
        input_output_aliases=aliases,
        compiler_params=pltpu.CompilerParams(vmem_limit_bytes=TERMS_VMEM),
        cost_estimate=pl.CostEstimate(
            flops=2 * size**3 * capacity * count, bytes_accessed=2**18, transcendentals=0
        ),
        name="terms",
    )(probe, left, right, *messages, *operands)
    return tuple(results) if state is None or last else (state[0], *results)


def finish_kernel(n_pos, n_obj, ring, steps, capacity, size, tile, acc, *rest):
    ends, rest = rest[: len(steps)], rest[len(steps) :]
    messages, (out, infos, chosen, sems) = rest[: len(ring)], rest[len(ring) :]
    loads = [
        pltpu.make_async_copy(message.at[pl.ds(capacity * size, INFO_ROWS)], infos.at[i], sems.at[i])
        for i, message in enumerate(messages)
    ]
    for load in loads:
        load.start()
    for load in loads:
        load.wait()
    _, rows, cols = tile.shape
    parts = cols // LANES
    each = rows // size
    me = lax.axis_index("pos")
    for side, neighbour in enumerate((lax.rem(me + n_pos - 1, n_pos), lax.rem(me + 1, n_pos))):
        block = jnp.zeros((INFO_ROWS, size), f32)
        for i, d in enumerate(ring):
            block = jnp.where(jnp.bitwise_xor(me, neighbour) == d, infos[i].astype(f32), block)
        chosen[side] = block

    def edge(side, plane):
        place = 1 + (2 * each if side == 0 else 0) + plane * each
        values = [chosen[side, place + i : place + i + 1, :] for i in range(each)]
        return jnp.concatenate([jnp.transpose(jnp.broadcast_to(v, (LANES, size))) for v in values], axis=0)

    level = lax.axis_index("obj")
    rim_at = ends[0].shape[1] - SUBLANES

    def end_row(side, plane, k):
        neighbour = lax.rem(level + (n_obj - 1 if side == 0 else 1), n_obj)
        place = rim_at + (rim_width(cols, size) if side == 0 else 0) + k * LANES // size
        lanes = slice(k * LANES % size, k * LANES % size + LANES)
        value = jnp.zeros((1, LANES), f32)
        for block, step in zip(ends, steps):
            value = jnp.where(jnp.bitwise_xor(level, neighbour) == step, block[plane, place : place + 1, lanes], value)
        return value

    lane = lax.broadcasted_iota(jnp.int32, (rows, LANES), 1)
    line = lax.broadcasted_iota(jnp.int32, (rows, LANES), 0)
    for plane in range(2):
        blocks = [tile[plane, :, k * LANES : (k + 1) * LANES] for k in range(parts)]
        to_right = [pltpu.roll(block, 1, 1) for block in blocks]
        to_left = [pltpu.roll(block, LANES - 1, 1) for block in blocks]
        low, high = edge(0, plane), edge(1, plane)
        for k in range(parts):
            here = slice(k * LANES, (k + 1) * LANES)
            block = blocks[k]
            near = jnp.where(lane == 0, to_right[k - 1] if k > 0 else low, to_right[k])
            near += jnp.where(lane == LANES - 1, to_left[k + 1] if k + 1 < parts else high, to_left[k])
            near += jnp.where(line == 0, end_row(0, plane, k), pltpu.roll(block, 1, 0))
            near += jnp.where(line == rows - 1, end_row(1, plane, k), pltpu.roll(block, rows - 1, 0))
            smooth = 4.0 * block - near
            out[plane, :, here] = block - 0.25 * (acc[plane * parts + k] + 0.5 * smooth)


def finish(tile, acc, steps, ends, ring, messages, n_pos, n_obj, capacity, size):
    full = pl.BlockSpec(memory_space=pltpu.VMEM)
    far = pl.BlockSpec(memory_space=pltpu.HBM)
    return pl.pallas_call(
        functools.partial(finish_kernel, n_pos, n_obj, ring, steps, capacity, size),
        in_specs=[full] * (2 + len(ends)) + [far] * len(ring),
        out_specs=full,
        out_shape=jax.ShapeDtypeStruct(tile.shape, f32),
        scratch_shapes=[
            pltpu.VMEM((len(ring), INFO_ROWS, size), bf16),
            pltpu.VMEM((2, INFO_ROWS, size), f32),
            pltpu.SemaphoreType.DMA((len(ring),)),
        ],
        compiler_params=pltpu.CompilerParams(vmem_limit_bytes=SMALL_VMEM),
        cost_estimate=pl.CostEstimate(flops=2**24, bytes_accessed=2**23, transcendentals=0),
        name="finish",
    )(tile, acc, *ends, *messages)


def small_call(body, name, operands, shapes):
    return pl.pallas_call(
        body,
        out_shape=shapes,
        compiler_params=pltpu.CompilerParams(vmem_limit_bytes=SMALL_VMEM),
        name=name,
    )(*operands)


def split_kernel(pairs, keep, got, *pieces):
    rows = pieces[0].shape[1]
    pair = lax.axis_index("pos") // 2
    for d in range(pairs):
        here = pl.ds(pl.multiple_of(jnp.bitwise_xor(pair, d) * rows, rows), rows)
        pieces[d][...] = keep[:, here, :] + got[:, here, :]


def join_kernel(pairs, scale, probe, *rest):
    pieces, out = rest[:pairs], rest[pairs]
    rows = pieces[0].shape[1]
    half = out.shape[1]
    me = lax.axis_index("pos")
    for d in range(pairs):
        start = jnp.bitwise_xor(me // 2, d) * rows
        old = probe[:, pl.ds(pl.multiple_of(lax.rem(me, 2) * half + start, rows), rows), :]
        out[:, pl.ds(pl.multiple_of(start, rows), rows), :] = old - pieces[d][...] * scale


def whole_kernel(mine, other, out):
    half = mine.shape[1]
    odd = lax.rem(lax.axis_index("pos"), 2)
    out[:, pl.ds(pl.multiple_of(odd * half, half), half), :] = mine[...]
    out[:, pl.ds(pl.multiple_of((1 - odd) * half, half), half), :] = other[...]


def step_probe(probe, keep, send, scale, rim, beside):
    n_pos = lax.axis_size("pos")
    n_obj = lax.axis_size("obj")
    pairs = n_pos // 2
    planes, half, size = keep.shape
    rows = half // pairs
    shape = jax.ShapeDtypeStruct((planes, rows, size), f32)
    got = exchange(send, "pos", 1)
    pieces = small_call(functools.partial(split_kernel, pairs), "split", (keep, got), [shape] * pairs)
    total = pieces[0]
    for d in range(1, pairs):
        total = total + exchange(pieces[d], "pos", 2 * d)
    steps, ends = [], []
    while 2 ** len(steps) < n_obj:
        got = exchange(jnp.concatenate([total, rim], axis=1), "obj", 2 ** len(steps))
        total = total + got[:, :rows]
        rim = got[:, rows:]
        steps.append(2 ** (len(steps) + 1) - 1)
        ends.append(got)
    gathered = [total] + [exchange(total, "pos", 2 * d) for d in range(1, pairs)]
    gathered, result = lax.optimization_barrier((gathered, beside(steps, ends)))
    mine = small_call(
        functools.partial(join_kernel, pairs, scale),
        "join",
        (probe, *gathered),
        jax.ShapeDtypeStruct(keep.shape, f32),
    )
    other = exchange(mine, "pos", 1)
    new_probe = small_call(whole_kernel, "whole", (mine, other), jax.ShapeDtypeStruct(probe.shape, f32))
    return new_probe, result


def shards(object_field, probe, amplitude, row_offset, col_offset, owner):
    n_pos = lax.axis_size("pos")
    n_obj = lax.axis_size("obj")
    pos_dev, size, _ = amplitude.shape
    capacity = max(2, pos_dev // n_pos + 1)
    left, right = (jnp.asarray(table) for table in dft_blocks(size))
    if n_pos == 8:
        early, later = [1, 2, 4, 3, 5], {4: [6], 3: [7]}
        order = [1, 0, 2, 4, 3, 5, 6, 7]
    else:
        window = 4
        order = [1, 0] + list(range(2, n_pos))
        early, later = list(range(1, 1 + window)), {d: [d + window] for d in range(1, n_pos - window)}
    *packed, rim = pack(
        owner, row_offset, col_offset, amplitude, object_field, n_pos, capacity, early + [d for d in order if d not in early]
    )
    received = {d: exchange(packed[d], "pos", d) for d in early}
    received[0] = packed[0]
    state = terms(probe, left, right, [received[order[0]]], capacity, source=object_field)
    for d in order[:-1]:
        if d != order[0]:
            state = terms(probe, left, right, [received[d]], capacity, state=state)
        for e in later.get(d, []):
            state, sending = lax.optimization_barrier((state, packed[e]))
            received[e] = exchange(sending, "pos", e)
    acc, keep, send = terms(probe, left, right, [received[order[-1]]], capacity, state=state, last=True)
    ring = sorted({i ^ ((i + 1) % n_pos) for i in range(n_pos)})
    near = [received[d] for d in ring]

    def object_step(steps, ends):
        return finish(object_field, acc, steps, ends, ring, near, n_pos, n_obj, capacity, size)

    scale = 1.0 / math.sqrt(pos_dev * n_pos * n_obj)
    new_probe, new_object = step_probe(probe, keep, send, scale, rim, object_step)
    return (new_object, new_probe)


def solution(mesh):
    placed = (
        P(None, "obj", "pos"),
        P(),
        P(("pos", "obj"), None, None),
        P(("pos", "obj")),
        P(("pos", "obj")),
        P(("pos", "obj")),
    )
    return jax.shard_map(
        shards, mesh=mesh, in_specs=placed, out_specs=(P(None, "obj", "pos"), P()), check_vma=False
    )
```

```python
import functools
import math

import jax
import jax.numpy as jnp
import numpy as np
from jax import lax
from jax.experimental import pallas as pl
from jax.experimental.pallas import tpu as pltpu
from jax.sharding import PartitionSpec as P

LANES = 128
INFO_ROWS = 16
SUBLANES = 8
PACK_VMEM = 60 * 2**20
SMALL_VMEM = 16 * 2**20
TERMS_VMEM = 32 * 2**20
bf16 = jnp.bfloat16
f32 = jnp.float32


def dft_blocks(size):
    index = np.arange(size, dtype=np.int32)
    product = index[:, None] * index[None, :] % size
    angle = product.astype(np.float32) * np.float32(2.0 * math.pi / size)
    scale = np.float32(1.0 / math.sqrt(size))
    real_part = (np.cos(angle) * scale).astype(bf16)
    imag_part = (-np.sin(angle) * scale).astype(bf16)
    left = np.block([[real_part, -imag_part], [imag_part, real_part]])
    right = np.block([[real_part, imag_part], [-imag_part, real_part]])
    return left, right


def exchange(value, axis, distance):
    count = lax.axis_size(axis)
    return lax.ppermute(value, axis, [(i, i ^ distance) for i in range(count)])


def dot(a, b):
    return jnp.dot(a, b, preferred_element_type=f32)


def rim_width(cols, size):
    return -(-cols // size)


def pack_kernel(n_pos, capacity, order, owner_in, row_in, col_in, amp_in, tile, *rest):
    outs, rim = rest[:n_pos], rest[n_pos]
    owner, row, col, counts, source, amp, sides, ends, edges, info, rim_rows = rest[n_pos + 1 : n_pos + 12]
    int_sems, amp_sem, side_sems, end_sems, out_sems, info_sems = rest[n_pos + 12 :]
    pos_dev, size, _ = amp_in.shape
    _, rows, cols = tile.shape
    int_loads = [
        pltpu.make_async_copy(src, dst, int_sems.at[i])
        for i, (src, dst) in enumerate(((owner_in, owner), (row_in, row), (col_in, col)))
    ]
    amp_load = pltpu.make_async_copy(amp_in, amp, amp_sem)
    side_loads = [
        pltpu.make_async_copy(tile.at[:, :, pl.ds(first, LANES)], sides.at[i], side_sems.at[i])
        for i, first in enumerate((0, cols - LANES))
    ]
    end_loads = [
        pltpu.make_async_copy(tile.at[:, pl.ds(first, SUBLANES), :], ends.at[i], end_sems.at[i])
        for i, first in enumerate((0, rows - SUBLANES))
    ]
    for load in int_loads + [amp_load] + end_loads + side_loads:
        load.start()
    me = lax.axis_index("pos")
    for slot in range(n_pos * capacity):
        source[slot] = 0
    for q in range(n_pos):
        counts[q] = 0
    for load in int_loads:
        load.wait()
    for item in range(pos_dev):
        who = owner[item]
        rank = counts[who]
        source[who * capacity + rank] = item
        counts[who] = rank + 1
    stores = []
    amp_load.wait()
    for d in order:
        partner = jnp.bitwise_xor(me, d)
        for k in range(capacity):
            item = source[partner * capacity + k]
            store = pltpu.make_async_copy(amp.at[item], outs[d].at[pl.ds(k * size, size)], out_sems.at[d, k])
            store.start()
            stores.append(store)
    edges[...] = jnp.zeros(edges.shape, f32)
    place = 1
    for i, lane_of_edge in enumerate((0, LANES - 1)):
        pick = (lax.broadcasted_iota(jnp.int32, (SUBLANES, LANES), 1) == lane_of_edge).astype(bf16)
        side_loads[i].wait()
        for plane in range(2):
            turned = lax.dot_general(
                pick, sides[i, plane].astype(bf16), (((1,), (1,)), ((), ())), preferred_element_type=f32
            )
            for part in range(rows // size):
                edges[place : place + 1, :] = turned[0:1, part * size : (part + 1) * size]
                place += 1
    edge_block = edges[...]
    lane = lax.broadcasted_iota(jnp.int32, (INFO_ROWS, size), 1)
    at_info = lax.broadcasted_iota(jnp.int32, (INFO_ROWS, size), 0) == 0
    for d in order:
        partner = jnp.bitwise_xor(me, d)
        held = counts[partner]
        block = jnp.zeros((INFO_ROWS, size), f32)
        for k in range(capacity):
            item = source[partner * capacity + k]
            for j, number in enumerate((row[item], col[item], (k < held).astype(jnp.int32))):
                block = jnp.where(lane == 3 * k + j, number.astype(f32), block)
        info[d] = jnp.where(at_info, block, edge_block).astype(bf16)
        store = pltpu.make_async_copy(info.at[d], outs[d].at[pl.ds(capacity * size, INFO_ROWS)], info_sems.at[d])
        store.start()
        stores.append(store)
    rim_rows[...] = jnp.zeros(rim_rows.shape, f32)
    for i, at in enumerate((0, SUBLANES - 1)):
        end_loads[i].wait()
        for plane in range(2):
            for part, first in enumerate(range(0, cols, size)):
                width = min(size, cols - first)
                place = i * rim_width(cols, size) + part
                rim_rows[plane, place : place + 1, :width] = ends[i, plane, at : at + 1, first : first + width]
    store = pltpu.make_async_copy(rim_rows, rim, end_sems.at[2])
    store.start()
    stores.append(store)
    for store in stores:
        store.wait()


def pack(owner, row, col, amplitude, tile, n_pos, capacity, order):
    pos_dev, size, _ = amplitude.shape
    _, rows, cols = tile.shape
    far = pl.BlockSpec(memory_space=pltpu.HBM)
    ints = pltpu.SMEM((pos_dev,), jnp.int32)
    return pl.pallas_call(
        functools.partial(pack_kernel, n_pos, capacity, order),
        in_specs=[far] * 5,
        out_specs=[far] * (n_pos + 1),
        out_shape=[jax.ShapeDtypeStruct((capacity * size + INFO_ROWS, size), bf16)] * n_pos
        + [jax.ShapeDtypeStruct((2, SUBLANES, size), f32)],
        scratch_shapes=[
            ints,
            ints,
            ints,
            pltpu.SMEM((n_pos,), jnp.int32),
            pltpu.SMEM((n_pos * capacity,), jnp.int32),
            pltpu.VMEM(amplitude.shape, bf16),
            pltpu.VMEM((2, 2, rows, LANES), f32),
            pltpu.VMEM((2, 2, SUBLANES, cols), f32),
            pltpu.VMEM((INFO_ROWS, size), f32),
            pltpu.VMEM((n_pos, INFO_ROWS, size), bf16),
            pltpu.VMEM((2, SUBLANES, size), f32),
            pltpu.SemaphoreType.DMA((3,)),
            pltpu.SemaphoreType.DMA,
            pltpu.SemaphoreType.DMA((2,)),
            pltpu.SemaphoreType.DMA((3,)),
            pltpu.SemaphoreType.DMA((n_pos, capacity)),
            pltpu.SemaphoreType.DMA((n_pos,)),
        ],
        compiler_params=pltpu.CompilerParams(vmem_limit_bytes=PACK_VMEM),
        cost_estimate=pl.CostEstimate(flops=2**20, bytes_accessed=2**20, transcendentals=0),
        name="pack",
    )(owner, row, col, amplitude, tile)


def read_info(block, count):
    lane = lax.broadcasted_iota(jnp.int32, block.shape, 1)
    first = lax.broadcasted_iota(jnp.int32, block.shape, 0) == 0
    values = block.astype(f32)
    return [jnp.sum(jnp.where(first & (lane == j), values, 0.0)).astype(jnp.int32) for j in range(count)]


def window(tile, plane, row, col, size, parts):
    shift = lax.rem(LANES - col, LANES)
    keep = lax.broadcasted_iota(jnp.int32, (size, LANES), 1) < LANES - col
    rolled = [pltpu.roll(tile[plane * parts + k, pl.ds(row, size), :], shift, 1) for k in range(size // LANES + 1)]
    return jnp.concatenate([jnp.where(keep, rolled[k], rolled[k + 1]) for k in range(size // LANES)], axis=1)


def add_window(acc, plane, row, col, value, size, parts):
    inner = size // LANES
    keep = lax.broadcasted_iota(jnp.int32, (size, LANES), 1) >= col
    zero = jnp.zeros((size, LANES), f32)
    rolled = [pltpu.roll(value[:, k * LANES : (k + 1) * LANES], lax.rem(col, LANES), 1) for k in range(inner)]
    for k in range(inner + 1):
        here = rolled[k] if k < inner else zero
        before = rolled[k - 1] if k > 0 else zero
        acc[plane * parts + k, pl.ds(row, size), :] += jnp.where(keep, here, before)


def side_by_side(stacked, size):
    return jnp.concatenate([stacked[:size], stacked[size:]], axis=1)


def buffer_terms(amp, amp_load, info, tile, probe, left, right, emit, term, capacity, size, parts):
    numbers = read_info(info, 3 * capacity)
    slots = [tuple(numbers[3 * k : 3 * k + 3]) for k in range(capacity)]
    probe_re = probe[0]
    probe_im = probe[1]
    patches, psis = [], []
    for row, col, _ in slots:
        patch_re = window(tile, 0, row, col, size, parts)
        patch_im = window(tile, 1, row, col, size, parts)
        patches.append((patch_re.astype(bf16), patch_im.astype(bf16)))
        psi_re = (probe_re * patch_re - probe_im * patch_im).astype(bf16)
        psi_im = (probe_re * patch_im + probe_im * patch_re).astype(bf16)
        psis.append(jnp.concatenate([psi_re, psi_im], axis=0))
    halves = [side_by_side(dot(left[...], psi).astype(bf16), size) for psi in psis]
    waves = [dot(half, right[...]) for half in halves]
    diffs = []
    amp_load.wait()
    for k, wave in enumerate(waves):
        wave_re = wave[:, :size]
        wave_im = wave[:, size:]
        square = wave_re * wave_re + wave_im * wave_im
        measured = amp[k * size : (k + 1) * size, :].astype(f32)
        factor = 1.0 - measured * lax.rsqrt(jnp.maximum(square, 0.25))
        diffs.append(jnp.concatenate([(wave_re * factor).astype(bf16), (wave_im * factor).astype(bf16)], axis=0))
    backs = [side_by_side(dot(right[...], diff).astype(bf16), size) for diff in diffs]
    chis = [dot(back, left[...]) for back in backs]
    sum_re = sum_im = 0.0
    for slot, ((row, col, valid), (patch_re, patch_im), chi) in enumerate(zip(slots, patches, chis)):
        weight = valid.astype(f32)
        chi_re = chi[:, :size] * weight
        chi_im = chi[:, size:] * weight
        emit(slot, 0, row, col, (probe_re * chi_re + probe_im * chi_im).astype(bf16))
        emit(slot, 1, row, col, (probe_re * chi_im - probe_im * chi_re).astype(bf16))
        patch_re = patch_re.astype(f32)
        patch_im = patch_im.astype(f32)
        sum_re += patch_re * chi_re + patch_im * chi_im
        sum_im += patch_re * chi_im - patch_im * chi_re
    term[0] += sum_re
    term[1] += sum_im


def terms_kernel(count, capacity, first, last, probe, left, right, *rest):
    size = probe.shape[1]
    held, infos, sems = rest[-3:]
    messages, rest = rest[:count], rest[count:-3]
    info_loads, amp_loads = [], []
    for i, message in enumerate(messages):
        info_rows = pl.ds(capacity * size, INFO_ROWS)
        amp_rows = pl.ds(0, capacity * size)
        info_loads.append(pltpu.make_async_copy(message.at[info_rows], infos.at[i], sems.at[i, 0]))
        amp_loads.append(pltpu.make_async_copy(message.at[amp_rows], held.at[i], sems.at[i, 1]))
    for load in info_loads + amp_loads:
        load.start()
    if first:
        source, tile, acc, term = rest
        parts = tile.shape[0] // 2
        for plane in range(2):
            for k in range(parts):
                block = source[plane, :, k * LANES : (k + 1) * LANES]
                tile[plane * parts + k] = block.astype(bf16).astype(f32)
        acc[...] = jnp.zeros(acc.shape, f32)
        term[...] = jnp.zeros(term.shape, f32)
    elif last:
        tile, term_in, grads, keep, send, term = rest
        parts = tile.shape[0] // 2
        term[...] = term_in[...]
    else:
        tile, acc_in, term_in, acc, term = rest
        parts = tile.shape[0] // 2
        acc[...] = acc_in[...]
        term[...] = term_in[...]

    def emit(slot, plane, row, col, grad):
        if last:
            grads[slot, plane] = grad
        else:
            add_window(acc, plane, row, col, grad.astype(f32), size, parts)

    for i in range(count):
        info_loads[i].wait()
        buffer_terms(
            held.at[i], amp_loads[i], infos[i], tile, probe, left, right, emit, term, capacity, size, parts
        )
    if last:
        half = size // 2
        odd = lax.rem(lax.axis_index("pos"), 2)
        keep[...] = term[:, pl.ds(pl.multiple_of(odd * half, half), half), :]
        send[...] = term[:, pl.ds(pl.multiple_of((1 - odd) * half, half), half), :]


def terms(probe, left, right, messages, capacity, source=None, state=None, last=False):
    size = probe.shape[1]
    count = len(messages)
    full = pl.BlockSpec(memory_space=pltpu.VMEM)
    far = pl.BlockSpec(memory_space=pltpu.HBM)
    scratch = [
        pltpu.VMEM((count, capacity * size, size), bf16),
        pltpu.VMEM((count, INFO_ROWS, size), bf16),
        pltpu.SemaphoreType.DMA((count, 2)),
    ]
    if state is None:
        _, rows, cols = source.shape
        blocks = jax.ShapeDtypeStruct((2 * cols // LANES, rows, LANES), f32)
        operands = (source,)
        shapes = [blocks, blocks, jax.ShapeDtypeStruct(probe.shape, f32)]
        aliases = {}
    else:
        tile, acc, term = state
        if last:
            operands = (tile, term)
            shapes = [jax.ShapeDtypeStruct((capacity, 2, size, size), bf16)]
            shapes += [jax.ShapeDtypeStruct((2, size // 2, size), f32)] * 2
            scratch = [pltpu.VMEM(term.shape, f32)] + scratch
            aliases = {}
        else:
            operands = state
            shapes = [jax.ShapeDtypeStruct(acc.shape, f32), jax.ShapeDtypeStruct(term.shape, f32)]
            aliases = {4 + count: 0, 5 + count: 1}
    results = pl.pallas_call(
        functools.partial(terms_kernel, count, capacity, state is None, last),
        in_specs=[full] * 3 + [far] * count + [full] * len(operands),
        out_specs=[full] * len(shapes),
        out_shape=shapes,
        scratch_shapes=scratch,
        input_output_aliases=aliases,
        compiler_params=pltpu.CompilerParams(vmem_limit_bytes=TERMS_VMEM),
        cost_estimate=pl.CostEstimate(
            flops=2 * size**3 * capacity * count, bytes_accessed=2**18, transcendentals=0
        ),
        name="terms",
    )(probe, left, right, *messages, *operands)
    return tuple(results) if state is None or last else (state[0], *results)


def add_kernel(capacity, message, grads, acc_in, acc, info, sem):
    _, _, size, _ = grads.shape
    parts = acc.shape[0] // 2
    load = pltpu.make_async_copy(message.at[pl.ds(capacity * size, INFO_ROWS)], info, sem)
    load.start()
    acc[...] = acc_in[...]
    load.wait()
    numbers = read_info(info[...], 3 * capacity)
    for slot in range(capacity):
        for plane in range(2):
            add_window(acc, plane, numbers[3 * slot], numbers[3 * slot + 1], grads[slot, plane].astype(f32), size, parts)


def add_grads(message, grads, acc):
    capacity, _, size, _ = grads.shape
    full = pl.BlockSpec(memory_space=pltpu.VMEM)
    return pl.pallas_call(
        functools.partial(add_kernel, capacity),
        in_specs=[pl.BlockSpec(memory_space=pltpu.HBM), full, full],
        out_specs=full,
        out_shape=jax.ShapeDtypeStruct(acc.shape, f32),
        scratch_shapes=[pltpu.VMEM((INFO_ROWS, size), bf16), pltpu.SemaphoreType.DMA],
        input_output_aliases={2: 0},
        compiler_params=pltpu.CompilerParams(vmem_limit_bytes=SMALL_VMEM),
        cost_estimate=pl.CostEstimate(flops=2**20, bytes_accessed=2**18, transcendentals=0),
        name="add",
    )(message, grads, acc)


def finish_kernel(n_pos, n_obj, ring, steps, capacity, size, tile, acc, *rest):
    ends, rest = rest[: len(steps)], rest[len(steps) :]
    messages, (out, infos, chosen, sems) = rest[: len(ring)], rest[len(ring) :]
    loads = [
        pltpu.make_async_copy(message.at[pl.ds(capacity * size, INFO_ROWS)], infos.at[i], sems.at[i])
        for i, message in enumerate(messages)
    ]
    for load in loads:
        load.start()
    for load in loads:
        load.wait()
    _, rows, cols = tile.shape
    parts = cols // LANES
    each = rows // size
    me = lax.axis_index("pos")
    for side, neighbour in enumerate((lax.rem(me + n_pos - 1, n_pos), lax.rem(me + 1, n_pos))):
        block = jnp.zeros((INFO_ROWS, size), f32)
        for i, d in enumerate(ring):
            block = jnp.where(jnp.bitwise_xor(me, neighbour) == d, infos[i].astype(f32), block)
        chosen[side] = block

    def edge(side, plane):
        place = 1 + (2 * each if side == 0 else 0) + plane * each
        values = [chosen[side, place + i : place + i + 1, :] for i in range(each)]
        return jnp.concatenate([jnp.transpose(jnp.broadcast_to(v, (LANES, size))) for v in values], axis=0)

    level = lax.axis_index("obj")
    rim_at = ends[0].shape[1] - SUBLANES

    def end_row(side, plane, k):
        neighbour = lax.rem(level + (n_obj - 1 if side == 0 else 1), n_obj)
        place = rim_at + (rim_width(cols, size) if side == 0 else 0) + k * LANES // size
        lanes = slice(k * LANES % size, k * LANES % size + LANES)
        value = jnp.zeros((1, LANES), f32)
        for block, step in zip(ends, steps):
            value = jnp.where(jnp.bitwise_xor(level, neighbour) == step, block[plane, place : place + 1, lanes], value)
        return value

    lane = lax.broadcasted_iota(jnp.int32, (rows, LANES), 1)
    line = lax.broadcasted_iota(jnp.int32, (rows, LANES), 0)
    for plane in range(2):
        blocks = [tile[plane, :, k * LANES : (k + 1) * LANES] for k in range(parts)]
        to_right = [pltpu.roll(block, 1, 1) for block in blocks]
        to_left = [pltpu.roll(block, LANES - 1, 1) for block in blocks]
        low, high = edge(0, plane), edge(1, plane)
        for k in range(parts):
            here = slice(k * LANES, (k + 1) * LANES)
            block = blocks[k]
            near = jnp.where(lane == 0, to_right[k - 1] if k > 0 else low, to_right[k])
            near += jnp.where(lane == LANES - 1, to_left[k + 1] if k + 1 < parts else high, to_left[k])
            near += jnp.where(line == 0, end_row(0, plane, k), pltpu.roll(block, 1, 0))
            near += jnp.where(line == rows - 1, end_row(1, plane, k), pltpu.roll(block, rows - 1, 0))
            smooth = 4.0 * block - near
            out[plane, :, here] = block - 0.25 * (acc[plane * parts + k] + 0.5 * smooth)


def finish(tile, acc, steps, ends, ring, messages, n_pos, n_obj, capacity, size):
    full = pl.BlockSpec(memory_space=pltpu.VMEM)
    far = pl.BlockSpec(memory_space=pltpu.HBM)
    return pl.pallas_call(
        functools.partial(finish_kernel, n_pos, n_obj, ring, steps, capacity, size),
        in_specs=[full] * (2 + len(ends)) + [far] * len(ring),
        out_specs=full,
        out_shape=jax.ShapeDtypeStruct(tile.shape, f32),
        scratch_shapes=[
            pltpu.VMEM((len(ring), INFO_ROWS, size), bf16),
            pltpu.VMEM((2, INFO_ROWS, size), f32),
            pltpu.SemaphoreType.DMA((len(ring),)),
        ],
        compiler_params=pltpu.CompilerParams(vmem_limit_bytes=SMALL_VMEM),
        cost_estimate=pl.CostEstimate(flops=2**24, bytes_accessed=2**23, transcendentals=0),
        name="finish",
    )(tile, acc, *ends, *messages)


def small_call(body, name, operands, shapes):
    return pl.pallas_call(
        body,
        out_shape=shapes,
        compiler_params=pltpu.CompilerParams(vmem_limit_bytes=SMALL_VMEM),
        name=name,
    )(*operands)


def split_kernel(pairs, keep, got, *pieces):
    rows = pieces[0].shape[1]
    pair = lax.axis_index("pos") // 2
    for d in range(pairs):
        here = pl.ds(pl.multiple_of(jnp.bitwise_xor(pair, d) * rows, rows), rows)
        pieces[d][...] = keep[:, here, :] + got[:, here, :]


def join_kernel(pairs, scale, probe, *rest):
    pieces, out = rest[:pairs], rest[pairs]
    rows = pieces[0].shape[1]
    half = out.shape[1]
    me = lax.axis_index("pos")
    for d in range(pairs):
        start = jnp.bitwise_xor(me // 2, d) * rows
        old = probe[:, pl.ds(pl.multiple_of(lax.rem(me, 2) * half + start, rows), rows), :]
        out[:, pl.ds(pl.multiple_of(start, rows), rows), :] = old - pieces[d][...] * scale


def whole_kernel(mine, other, out):
    half = mine.shape[1]
    odd = lax.rem(lax.axis_index("pos"), 2)
    out[:, pl.ds(pl.multiple_of(odd * half, half), half), :] = mine[...]
    out[:, pl.ds(pl.multiple_of((1 - odd) * half, half), half), :] = other[...]


def step_probe(probe, keep, send, scale, rim, acc, beside):
    n_pos = lax.axis_size("pos")
    n_obj = lax.axis_size("obj")
    pairs = n_pos // 2
    planes, half, size = keep.shape
    rows = half // pairs
    shape = jax.ShapeDtypeStruct((planes, rows, size), f32)
    got = exchange(send, "pos", 1)
    pieces = small_call(functools.partial(split_kernel, pairs), "split", (keep, got), [shape] * pairs)
    total = pieces[0]
    for d in reversed(range(1, pairs)):
        total = total + exchange(pieces[d], "pos", 2 * d)
    steps, ends = [], []
    while 2 ** len(steps) < n_obj:
        got = exchange(jnp.concatenate([total, rim], axis=1), "obj", 2 ** len(steps))
        if not steps:
            got, acc = lax.optimization_barrier((got, acc))
        total = total + got[:, :rows]
        rim = got[:, rows:]
        steps.append(2 ** (len(steps) + 1) - 1)
        ends.append(got)
    gathered = [total] + [exchange(total, "pos", 2 * d) for d in range(1, pairs)]
    gathered, result = lax.optimization_barrier((gathered, beside(acc, steps, ends)))
    mine = small_call(
        functools.partial(join_kernel, pairs, scale),
        "join",
        (probe, *gathered),
        jax.ShapeDtypeStruct(keep.shape, f32),
    )
    other = exchange(mine, "pos", 1)
    new_probe = small_call(whole_kernel, "whole", (mine, other), jax.ShapeDtypeStruct(probe.shape, f32))
    return new_probe, result


def shards(object_field, probe, amplitude, row_offset, col_offset, owner):
    n_pos = lax.axis_size("pos")
    n_obj = lax.axis_size("obj")
    pos_dev, size, _ = amplitude.shape
    capacity = max(2, pos_dev // n_pos + 1)
    left, right = (jnp.asarray(table) for table in dft_blocks(size))
    if n_pos == 8:
        early, later = [1, 2, 4, 3, 5], {4: [6], 3: [7]}
        order = [1, 0, 2, 4, 3, 5, 6, 7]
    else:
        window = 4
        order = [1, 0] + list(range(2, n_pos))
        early, later = list(range(1, 1 + window)), {d: [d + window] for d in range(1, n_pos - window)}
    *packed, rim = pack(
        owner, row_offset, col_offset, amplitude, object_field, n_pos, capacity, early + [d for d in order if d not in early]
    )
    received = {d: exchange(packed[d], "pos", d) for d in early}
    received[0] = packed[0]
    state = terms(probe, left, right, [received[order[0]]], capacity, source=object_field)
    for d in order[:-1]:
        if d != order[0]:
            state = terms(probe, left, right, [received[d]], capacity, state=state)
        for e in later.get(d, []):
            state, sending = lax.optimization_barrier((state, packed[e]))
            received[e] = exchange(sending, "pos", e)
    grads, keep, send = terms(probe, left, right, [received[order[-1]]], capacity, state=state, last=True)
    acc = add_grads(received[order[-1]], grads, state[1])
    ring = sorted({i ^ ((i + 1) % n_pos) for i in range(n_pos)})
    near = [received[d] for d in ring]

    def object_step(acc, steps, ends):
        return finish(object_field, acc, steps, ends, ring, near, n_pos, n_obj, capacity, size)

    scale = 1.0 / math.sqrt(pos_dev * n_pos * n_obj)
    new_probe, new_object = step_probe(probe, keep, send, scale, rim, acc, object_step)
    return (new_object, new_probe)


def solution(mesh):
    placed = (
        P(None, "obj", "pos"),
        P(),
        P(("pos", "obj"), None, None),
        P(("pos", "obj")),
        P(("pos", "obj")),
        P(("pos", "obj")),
    )
    return jax.shard_map(
        shards, mesh=mesh, in_specs=placed, out_specs=(P(None, "obj", "pos"), P()), check_vma=False
    )
```

```python
import functools
import math

import jax
import jax.numpy as jnp
import numpy as np
from jax import lax
from jax.experimental import pallas as pl
from jax.experimental.pallas import tpu as pltpu
from jax.sharding import PartitionSpec as P

LANES = 128
INFO_ROWS = 16
SUBLANES = 8
PACK_VMEM = 60 * 2**20
SMALL_VMEM = 16 * 2**20
TERMS_VMEM = 32 * 2**20
bf16 = jnp.bfloat16
f32 = jnp.float32


def dft_blocks(size):
    index = np.arange(size, dtype=np.int32)
    product = index[:, None] * index[None, :] % size
    angle = product.astype(np.float32) * np.float32(2.0 * math.pi / size)
    scale = np.float32(1.0 / math.sqrt(size))
    real_part = (np.cos(angle) * scale).astype(bf16)
    imag_part = (-np.sin(angle) * scale).astype(bf16)
    left = np.block([[real_part, -imag_part], [imag_part, real_part]])
    right = np.block([[real_part, imag_part], [-imag_part, real_part]])
    return left, right


def exchange(value, axis, distance):
    count = lax.axis_size(axis)
    return lax.ppermute(value, axis, [(i, i ^ distance) for i in range(count)])


def dot(a, b):
    return jnp.dot(a, b, preferred_element_type=f32)


def rim_width(cols, size):
    return -(-cols // size)


def pack_kernel(n_pos, capacity, order, owner_in, row_in, col_in, amp_in, tile, *rest):
    outs, rim = rest[:n_pos], rest[n_pos]
    owner, row, col, counts, source, amp, sides, ends, edges, info, rim_rows = rest[n_pos + 1 : n_pos + 12]
    int_sems, amp_sem, side_sems, end_sems, out_sems, info_sems = rest[n_pos + 12 :]
    pos_dev, size, _ = amp_in.shape
    _, rows, cols = tile.shape
    int_loads = [
        pltpu.make_async_copy(src, dst, int_sems.at[i])
        for i, (src, dst) in enumerate(((owner_in, owner), (row_in, row), (col_in, col)))
    ]
    amp_load = pltpu.make_async_copy(amp_in, amp, amp_sem)
    side_loads = [
        pltpu.make_async_copy(tile.at[:, :, pl.ds(first, LANES)], sides.at[i], side_sems.at[i])
        for i, first in enumerate((0, cols - LANES))
    ]
    end_loads = [
        pltpu.make_async_copy(tile.at[:, pl.ds(first, SUBLANES), :], ends.at[i], end_sems.at[i])
        for i, first in enumerate((0, rows - SUBLANES))
    ]
    for load in int_loads + [amp_load] + end_loads + side_loads:
        load.start()
    me = lax.axis_index("pos")
    for slot in range(n_pos * capacity):
        source[slot] = 0
    for q in range(n_pos):
        counts[q] = 0
    for load in int_loads:
        load.wait()
    for item in range(pos_dev):
        who = owner[item]
        rank = counts[who]
        source[who * capacity + rank] = item
        counts[who] = rank + 1
    stores = []
    amp_load.wait()
    for d in order:
        partner = jnp.bitwise_xor(me, d)
        for k in range(capacity):
            item = source[partner * capacity + k]
            store = pltpu.make_async_copy(amp.at[item], outs[d].at[pl.ds(k * size, size)], out_sems.at[d, k])
            store.start()
            stores.append(store)
    edges[...] = jnp.zeros(edges.shape, f32)
    place = 1
    for i, lane_of_edge in enumerate((0, LANES - 1)):
        pick = (lax.broadcasted_iota(jnp.int32, (SUBLANES, LANES), 1) == lane_of_edge).astype(bf16)
        side_loads[i].wait()
        for plane in range(2):
            turned = lax.dot_general(
                pick, sides[i, plane].astype(bf16), (((1,), (1,)), ((), ())), preferred_element_type=f32
            )
            for part in range(rows // size):
                edges[place : place + 1, :] = turned[0:1, part * size : (part + 1) * size]
                place += 1
    edge_block = edges[...]
    lane = lax.broadcasted_iota(jnp.int32, (INFO_ROWS, size), 1)
    at_info = lax.broadcasted_iota(jnp.int32, (INFO_ROWS, size), 0) == 0
    for d in order:
        partner = jnp.bitwise_xor(me, d)
        held = counts[partner]
        block = jnp.zeros((INFO_ROWS, size), f32)
        for k in range(capacity):
            item = source[partner * capacity + k]
            for j, number in enumerate((row[item], col[item], (k < held).astype(jnp.int32))):
                block = jnp.where(lane == 3 * k + j, number.astype(f32), block)
        info[d] = jnp.where(at_info, block, edge_block).astype(bf16)
        store = pltpu.make_async_copy(info.at[d], outs[d].at[pl.ds(capacity * size, INFO_ROWS)], info_sems.at[d])
        store.start()
        stores.append(store)
    rim_rows[...] = jnp.zeros(rim_rows.shape, f32)
    for i, at in enumerate((0, SUBLANES - 1)):
        end_loads[i].wait()
        for plane in range(2):
            for part, first in enumerate(range(0, cols, size)):
                width = min(size, cols - first)
                place = (2 * i + plane) * rim_width(cols, size) + part
                rim_rows[place : place + 1, :width] = ends[i, plane, at : at + 1, first : first + width]
    store = pltpu.make_async_copy(rim_rows, rim, end_sems.at[2])
    store.start()
    stores.append(store)
    for store in stores:
        store.wait()


def pack(owner, row, col, amplitude, tile, n_pos, capacity, order):
    pos_dev, size, _ = amplitude.shape
    _, rows, cols = tile.shape
    far = pl.BlockSpec(memory_space=pltpu.HBM)
    ints = pltpu.SMEM((pos_dev,), jnp.int32)
    rim_shape = (-(-4 * rim_width(cols, size) // SUBLANES) * SUBLANES, size)
    return pl.pallas_call(
        functools.partial(pack_kernel, n_pos, capacity, order),
        in_specs=[far] * 5,
        out_specs=[far] * (n_pos + 1),
        out_shape=[jax.ShapeDtypeStruct((capacity * size + INFO_ROWS, size), bf16)] * n_pos
        + [jax.ShapeDtypeStruct(rim_shape, f32)],
        scratch_shapes=[
            ints,
            ints,
            ints,
            pltpu.SMEM((n_pos,), jnp.int32),
            pltpu.SMEM((n_pos * capacity,), jnp.int32),
            pltpu.VMEM(amplitude.shape, bf16),
            pltpu.VMEM((2, 2, rows, LANES), f32),
            pltpu.VMEM((2, 2, SUBLANES, cols), f32),
            pltpu.VMEM((INFO_ROWS, size), f32),
            pltpu.VMEM((n_pos, INFO_ROWS, size), bf16),
            pltpu.VMEM(rim_shape, f32),
            pltpu.SemaphoreType.DMA((3,)),
            pltpu.SemaphoreType.DMA,
            pltpu.SemaphoreType.DMA((2,)),
            pltpu.SemaphoreType.DMA((3,)),
            pltpu.SemaphoreType.DMA((n_pos, capacity)),
            pltpu.SemaphoreType.DMA((n_pos,)),
        ],
        compiler_params=pltpu.CompilerParams(vmem_limit_bytes=PACK_VMEM),
        cost_estimate=pl.CostEstimate(flops=2**20, bytes_accessed=2**20, transcendentals=0),
        name="pack",
    )(owner, row, col, amplitude, tile)


def read_info(block, count):
    lane = lax.broadcasted_iota(jnp.int32, block.shape, 1)
    first = lax.broadcasted_iota(jnp.int32, block.shape, 0) == 0
    values = block.astype(f32)
    return [jnp.sum(jnp.where(first & (lane == j), values, 0.0)).astype(jnp.int32) for j in range(count)]


def window(tile, plane, row, col, size, parts):
    shift = lax.rem(LANES - col, LANES)
    keep = lax.broadcasted_iota(jnp.int32, (size, LANES), 1) < LANES - col
    rolled = [pltpu.roll(tile[plane * parts + k, pl.ds(row, size), :], shift, 1) for k in range(size // LANES + 1)]
    return jnp.concatenate([jnp.where(keep, rolled[k], rolled[k + 1]) for k in range(size // LANES)], axis=1)


def add_window(acc, plane, row, col, value, size, parts):
    inner = size // LANES
    keep = lax.broadcasted_iota(jnp.int32, (size, LANES), 1) >= col
    zero = jnp.zeros((size, LANES), f32)
    rolled = [pltpu.roll(value[:, k * LANES : (k + 1) * LANES], lax.rem(col, LANES), 1) for k in range(inner)]
    for k in range(inner + 1):
        here = rolled[k] if k < inner else zero
        before = rolled[k - 1] if k > 0 else zero
        acc[plane * parts + k, pl.ds(row, size), :] += jnp.where(keep, here, before)


def side_by_side(stacked, size):
    return jnp.concatenate([stacked[:size], stacked[size:]], axis=1)


def buffer_terms(amp, tile, probe, left, right, emit, term, capacity, size, parts):
    numbers = read_info(amp[capacity * size :, :], 3 * capacity)
    slots = [tuple(numbers[3 * k : 3 * k + 3]) for k in range(capacity)]
    probe_re = probe[0]
    probe_im = probe[1]
    patches, psis = [], []
    for row, col, _ in slots:
        patch_re = window(tile, 0, row, col, size, parts)
        patch_im = window(tile, 1, row, col, size, parts)
        patches.append((patch_re.astype(bf16), patch_im.astype(bf16)))
        psi_re = (probe_re * patch_re - probe_im * patch_im).astype(bf16)
        psi_im = (probe_re * patch_im + probe_im * patch_re).astype(bf16)
        psis.append(jnp.concatenate([psi_re, psi_im], axis=0))
    halves = [side_by_side(dot(left[...], psi).astype(bf16), size) for psi in psis]
    waves = [dot(half, right[...]) for half in halves]
    diffs = []
    for k, wave in enumerate(waves):
        wave_re = wave[:, :size]
        wave_im = wave[:, size:]
        square = wave_re * wave_re + wave_im * wave_im
        measured = amp[k * size : (k + 1) * size, :].astype(f32)
        factor = 1.0 - measured * lax.rsqrt(jnp.maximum(square, 0.25))
        diffs.append(jnp.concatenate([(wave_re * factor).astype(bf16), (wave_im * factor).astype(bf16)], axis=0))
    backs = [side_by_side(dot(right[...], diff).astype(bf16), size) for diff in diffs]
    chis = [dot(back, left[...]) for back in backs]
    sum_re = sum_im = 0.0
    for slot, ((row, col, valid), (patch_re, patch_im), chi) in enumerate(zip(slots, patches, chis)):
        weight = valid.astype(f32)
        chi_re = chi[:, :size] * weight
        chi_im = chi[:, size:] * weight
        emit(slot, 0, row, col, (probe_re * chi_re + probe_im * chi_im).astype(bf16))
        emit(slot, 1, row, col, (probe_re * chi_im - probe_im * chi_re).astype(bf16))
        patch_re = patch_re.astype(f32)
        patch_im = patch_im.astype(f32)
        sum_re += patch_re * chi_re + patch_im * chi_im
        sum_im += patch_re * chi_im - patch_im * chi_re
    term[0] += sum_re
    term[1] += sum_im


def terms_kernel(count, capacity, first, last, probe, left, right, *rest):
    size = probe.shape[1]
    messages, rest = rest[:count], rest[count:]
    if first:
        source, tile, acc, term = rest
        parts = tile.shape[0] // 2
        for plane in range(2):
            for k in range(parts):
                block = source[plane, :, k * LANES : (k + 1) * LANES]
                tile[plane * parts + k] = block.astype(bf16).astype(f32)
        acc[...] = jnp.zeros(acc.shape, f32)
        term[...] = jnp.zeros(term.shape, f32)
    elif last:
        tile, term_in, grads, keep, send, term = rest
        parts = tile.shape[0] // 2
        term[...] = term_in[...]
    else:
        tile, acc_in, term_in, acc, term = rest
        parts = tile.shape[0] // 2
        acc[...] = acc_in[...]
        term[...] = term_in[...]

    def emit(slot, plane, row, col, grad):
        if last:
            grads[slot, plane] = grad
        else:
            add_window(acc, plane, row, col, grad.astype(f32), size, parts)

    for message in messages:
        buffer_terms(message, tile, probe, left, right, emit, term, capacity, size, parts)
    if last:
        half = size // 2
        odd = lax.rem(lax.axis_index("pos"), 2)
        keep[...] = term[:, pl.ds(pl.multiple_of(odd * half, half), half), :]
        send[...] = term[:, pl.ds(pl.multiple_of((1 - odd) * half, half), half), :]


def terms(probe, left, right, messages, capacity, source=None, state=None, last=False):
    size = probe.shape[1]
    count = len(messages)
    full = pl.BlockSpec(memory_space=pltpu.VMEM)
    scratch = []
    if state is None:
        _, rows, cols = source.shape
        blocks = jax.ShapeDtypeStruct((2 * cols // LANES, rows, LANES), f32)
        operands = (source,)
        shapes = [blocks, blocks, jax.ShapeDtypeStruct(probe.shape, f32)]
        aliases = {}
    else:
        tile, acc, term = state
        if last:
            operands = (tile, term)
            shapes = [jax.ShapeDtypeStruct((capacity, 2, size, size), bf16)]
            shapes += [jax.ShapeDtypeStruct((2, size // 2, size), f32)] * 2
            scratch = [pltpu.VMEM(term.shape, f32)]
            aliases = {}
        else:
            operands = state
            shapes = [jax.ShapeDtypeStruct(acc.shape, f32), jax.ShapeDtypeStruct(term.shape, f32)]
            aliases = {4 + count: 0, 5 + count: 1}
    results = pl.pallas_call(
        functools.partial(terms_kernel, count, capacity, state is None, last),
        in_specs=[full] * (3 + count + len(operands)),
        out_specs=[full] * len(shapes),
        out_shape=shapes,
        scratch_shapes=scratch,
        input_output_aliases=aliases,
        compiler_params=pltpu.CompilerParams(vmem_limit_bytes=TERMS_VMEM),
        cost_estimate=pl.CostEstimate(
            flops=2 * size**3 * capacity * count, bytes_accessed=2**18, transcendentals=0
        ),
        name="terms",
    )(probe, left, right, *messages, *operands)
    return tuple(results) if state is None or last else (state[0], *results)


def add_kernel(capacity, message, grads, acc_in, acc, info, sem):
    _, _, size, _ = grads.shape
    parts = acc.shape[0] // 2
    load = pltpu.make_async_copy(message.at[pl.ds(capacity * size, INFO_ROWS)], info, sem)
    load.start()
    acc[...] = acc_in[...]
    load.wait()
    numbers = read_info(info[...], 3 * capacity)
    for slot in range(capacity):
        for plane in range(2):
            add_window(acc, plane, numbers[3 * slot], numbers[3 * slot + 1], grads[slot, plane].astype(f32), size, parts)


def add_grads(message, grads, acc):
    capacity, _, size, _ = grads.shape
    full = pl.BlockSpec(memory_space=pltpu.VMEM)
    return pl.pallas_call(
        functools.partial(add_kernel, capacity),
        in_specs=[pl.BlockSpec(memory_space=pltpu.HBM), full, full],
        out_specs=full,
        out_shape=jax.ShapeDtypeStruct(acc.shape, f32),
        scratch_shapes=[pltpu.VMEM((INFO_ROWS, size), bf16), pltpu.SemaphoreType.DMA],
        input_output_aliases={2: 0},
        compiler_params=pltpu.CompilerParams(vmem_limit_bytes=SMALL_VMEM),
        cost_estimate=pl.CostEstimate(flops=2**20, bytes_accessed=2**18, transcendentals=0),
        name="add",
    )(message, grads, acc)


def finish_kernel(n_pos, n_obj, ring, steps, capacity, size, tile, acc, *rest):
    ends, rest = rest[: len(steps)], rest[len(steps) :]
    messages, (out, infos, chosen, sems) = rest[: len(ring)], rest[len(ring) :]
    loads = [
        pltpu.make_async_copy(message.at[pl.ds(capacity * size, INFO_ROWS)], infos.at[i], sems.at[i])
        for i, message in enumerate(messages)
    ]
    for load in loads:
        load.start()
    for load in loads:
        load.wait()
    _, rows, cols = tile.shape
    parts = cols // LANES
    each = rows // size
    me = lax.axis_index("pos")
    for side, neighbour in enumerate((lax.rem(me + n_pos - 1, n_pos), lax.rem(me + 1, n_pos))):
        block = jnp.zeros((INFO_ROWS, size), f32)
        for i, d in enumerate(ring):
            block = jnp.where(jnp.bitwise_xor(me, neighbour) == d, infos[i].astype(f32), block)
        chosen[side] = block

    def edge(side, plane):
        place = 1 + (2 * each if side == 0 else 0) + plane * each
        values = [chosen[side, place + i : place + i + 1, :] for i in range(each)]
        return jnp.concatenate([jnp.transpose(jnp.broadcast_to(v, (LANES, size))) for v in values], axis=0)

    level = lax.axis_index("obj")
    rim_at = 2 * size // n_pos

    def end_row(side, plane, k):
        neighbour = lax.rem(level + (n_obj - 1 if side == 0 else 1), n_obj)
        place = rim_at + (2 * (1 - side) + plane) * rim_width(cols, size) + k * LANES // size
        lanes = slice(k * LANES % size, k * LANES % size + LANES)
        value = jnp.zeros((1, LANES), f32)
        for block, step in zip(ends, steps):
            value = jnp.where(jnp.bitwise_xor(level, neighbour) == step, block[place : place + 1, lanes], value)
        return value

    lane = lax.broadcasted_iota(jnp.int32, (rows, LANES), 1)
    line = lax.broadcasted_iota(jnp.int32, (rows, LANES), 0)
    for plane in range(2):
        blocks = [tile[plane, :, k * LANES : (k + 1) * LANES] for k in range(parts)]
        to_right = [pltpu.roll(block, 1, 1) for block in blocks]
        to_left = [pltpu.roll(block, LANES - 1, 1) for block in blocks]
        low, high = edge(0, plane), edge(1, plane)
        for k in range(parts):
            here = slice(k * LANES, (k + 1) * LANES)
            block = blocks[k]
            near = jnp.where(lane == 0, to_right[k - 1] if k > 0 else low, to_right[k])
            near += jnp.where(lane == LANES - 1, to_left[k + 1] if k + 1 < parts else high, to_left[k])
            near += jnp.where(line == 0, end_row(0, plane, k), pltpu.roll(block, 1, 0))
            near += jnp.where(line == rows - 1, end_row(1, plane, k), pltpu.roll(block, rows - 1, 0))
            smooth = 4.0 * block - near
            out[plane, :, here] = block - 0.25 * (acc[plane * parts + k] + 0.5 * smooth)


def finish(tile, acc, steps, ends, ring, messages, n_pos, n_obj, capacity, size):
    full = pl.BlockSpec(memory_space=pltpu.VMEM)
    far = pl.BlockSpec(memory_space=pltpu.HBM)
    return pl.pallas_call(
        functools.partial(finish_kernel, n_pos, n_obj, ring, steps, capacity, size),
        in_specs=[full] * (2 + len(ends)) + [far] * len(ring),
        out_specs=full,
        out_shape=jax.ShapeDtypeStruct(tile.shape, f32),
        scratch_shapes=[
            pltpu.VMEM((len(ring), INFO_ROWS, size), bf16),
            pltpu.VMEM((2, INFO_ROWS, size), f32),
            pltpu.SemaphoreType.DMA((len(ring),)),
        ],
        compiler_params=pltpu.CompilerParams(vmem_limit_bytes=SMALL_VMEM),
        cost_estimate=pl.CostEstimate(flops=2**24, bytes_accessed=2**23, transcendentals=0),
        name="finish",
    )(tile, acc, *ends, *messages)


def small_call(body, name, operands, shapes):
    return pl.pallas_call(
        body,
        out_shape=shapes,
        compiler_params=pltpu.CompilerParams(vmem_limit_bytes=SMALL_VMEM),
        name=name,
    )(*operands)


def split_kernel(pairs, keep, got, *pieces):
    rows = pieces[0].shape[1]
    pair = lax.axis_index("pos") // 2
    for d in range(pairs):
        here = pl.ds(pl.multiple_of(jnp.bitwise_xor(pair, d) * rows, rows), rows)
        pieces[d][...] = keep[:, here, :] + got[:, here, :]


def join_kernel(pairs, scale, probe, *rest):
    pieces, out = rest[:pairs], rest[pairs]
    rows = pieces[0].shape[1]
    half = out.shape[1]
    me = lax.axis_index("pos")
    for d in range(pairs):
        start = jnp.bitwise_xor(me // 2, d) * rows
        old = probe[:, pl.ds(pl.multiple_of(lax.rem(me, 2) * half + start, rows), rows), :]
        out[:, pl.ds(pl.multiple_of(start, rows), rows), :] = old - pieces[d][...] * scale


def whole_kernel(mine, other, out, sems):
    half = mine.shape[1]
    odd = lax.rem(lax.axis_index("pos"), 2)
    copies = [
        pltpu.make_async_copy(value, out.at[:, pl.ds(pl.multiple_of(which * half, half), half), :], sems.at[i])
        for i, (value, which) in enumerate(((mine, odd), (other, 1 - odd)))
    ]
    for copy in copies:
        copy.start()
    for copy in copies:
        copy.wait()


def whole(mine, other):
    planes, half, size = mine.shape
    full = pl.BlockSpec(memory_space=pltpu.VMEM)
    return pl.pallas_call(
        whole_kernel,
        in_specs=[full, full],
        out_specs=pl.BlockSpec(memory_space=pltpu.HBM),
        out_shape=jax.ShapeDtypeStruct((planes, 2 * half, size), f32),
        scratch_shapes=[pltpu.SemaphoreType.DMA((2,))],
        compiler_params=pltpu.CompilerParams(vmem_limit_bytes=SMALL_VMEM),
        name="whole",
    )(mine, other)


def step_probe(probe, keep, send, scale, rim, acc, beside):
    n_pos = lax.axis_size("pos")
    n_obj = lax.axis_size("obj")
    pairs = n_pos // 2
    planes, half, size = keep.shape
    rows = half // pairs
    shape = jax.ShapeDtypeStruct((planes, rows, size), f32)
    got = exchange(send, "pos", 1)
    pieces = small_call(functools.partial(split_kernel, pairs), "split", (keep, got), [shape] * pairs)
    total = pieces[0]
    for d in reversed(range(1, pairs)):
        total = total + exchange(pieces[d], "pos", 2 * d)
    steps, ends = [], []
    while 2 ** len(steps) < n_obj:
        flat = total.reshape(planes * rows, size)
        got = exchange(jnp.concatenate([flat, rim]), "obj", 2 ** len(steps))
        if not steps:
            got, acc = lax.optimization_barrier((got, acc))
        total = total + got[: planes * rows].reshape(total.shape)
        rim = got[planes * rows :]
        steps.append(2 ** (len(steps) + 1) - 1)
        ends.append(got)
    gathered = [total] + [exchange(total, "pos", 2 * d) for d in range(1, pairs)]
    gathered, result = lax.optimization_barrier((gathered, beside(acc, steps, ends)))
    mine = small_call(
        functools.partial(join_kernel, pairs, scale),
        "join",
        (probe, *gathered),
        jax.ShapeDtypeStruct(keep.shape, f32),
    )
    other = exchange(mine, "pos", 1)
    new_probe = whole(mine, other)
    return new_probe, result


def shards(object_field, probe, amplitude, row_offset, col_offset, owner):
    n_pos = lax.axis_size("pos")
    n_obj = lax.axis_size("obj")
    pos_dev, size, _ = amplitude.shape
    capacity = max(2, pos_dev // n_pos + 1)
    left, right = (jnp.asarray(table) for table in dft_blocks(size))
    if n_pos == 8:
        early, later = [1, 2, 4, 3, 5], {4: [6], 3: [7]}
        order = [1, 0, 2, 4, 3, 5, 6, 7]
    else:
        window = 4
        order = [1, 0] + list(range(2, n_pos))
        early, later = list(range(1, 1 + window)), {d: [d + window] for d in range(1, n_pos - window)}
    *packed, rim = pack(
        owner, row_offset, col_offset, amplitude, object_field, n_pos, capacity, early + [d for d in order if d not in early]
    )
    received = {d: exchange(packed[d], "pos", d) for d in early}
    received[0] = packed[0]
    state = terms(probe, left, right, [received[order[0]]], capacity, source=object_field)
    for d in order[:-1]:
        if d != order[0]:
            state = terms(probe, left, right, [received[d]], capacity, state=state)
        for e in later.get(d, []):
            state, sending = lax.optimization_barrier((state, packed[e]))
            received[e] = exchange(sending, "pos", e)
    grads, keep, send = terms(probe, left, right, [received[order[-1]]], capacity, state=state, last=True)
    acc = add_grads(received[order[-1]], grads, state[1])
    ring = sorted({i ^ ((i + 1) % n_pos) for i in range(n_pos)})
    near = [received[d] for d in ring]

    def object_step(acc, steps, ends):
        return finish(object_field, acc, steps, ends, ring, near, n_pos, n_obj, capacity, size)

    scale = 1.0 / math.sqrt(pos_dev * n_pos * n_obj)
    new_probe, new_object = step_probe(probe, keep, send, scale, rim, acc, object_step)
    return (new_object, new_probe)


def solution(mesh):
    placed = (
        P(None, "obj", "pos"),
        P(),
        P(("pos", "obj"), None, None),
        P(("pos", "obj")),
        P(("pos", "obj")),
        P(("pos", "obj")),
    )
    return jax.shard_map(
        shards, mesh=mesh, in_specs=placed, out_specs=(P(None, "obj", "pos"), P()), check_vma=False
    )
```

```python
import functools
import math

import jax
import jax.numpy as jnp
import numpy as np
from jax import lax
from jax.experimental import pallas as pl
from jax.experimental.pallas import tpu as pltpu
from jax.sharding import PartitionSpec as P

LANES = 128
INFO_ROWS = 16
SUBLANES = 8
PACK_VMEM = 60 * 2**20
SMALL_VMEM = 16 * 2**20
TERMS_VMEM = 32 * 2**20
bf16 = jnp.bfloat16
f32 = jnp.float32


def dft_blocks(size):
    index = np.arange(size, dtype=np.int32)
    product = index[:, None] * index[None, :] % size
    angle = product.astype(np.float32) * np.float32(2.0 * math.pi / size)
    scale = np.float32(1.0 / math.sqrt(size))
    real_part = (np.cos(angle) * scale).astype(bf16)
    imag_part = (-np.sin(angle) * scale).astype(bf16)
    left = np.block([[real_part, -imag_part], [imag_part, real_part]])
    right = np.block([[real_part, imag_part], [-imag_part, real_part]])
    return left, right


def exchange(value, axis, distance):
    count = lax.axis_size(axis)
    return lax.ppermute(value, axis, [(i, i ^ distance) for i in range(count)])


def dot(a, b):
    return jnp.dot(a, b, preferred_element_type=f32)


def rim_width(cols, size):
    return -(-cols // size)


def pack_kernel(n_pos, capacity, order, owner_in, row_in, col_in, amp_in, tile, *rest):
    outs, rim = rest[:n_pos], rest[n_pos]
    owner, row, col, counts, source, amp, sides, ends, edges, info, rim_rows = rest[n_pos + 1 : n_pos + 12]
    int_sems, amp_sem, side_sems, end_sems, out_sems, info_sems = rest[n_pos + 12 :]
    pos_dev, size, _ = amp_in.shape
    _, rows, cols = tile.shape
    int_loads = [
        pltpu.make_async_copy(src, dst, int_sems.at[i])
        for i, (src, dst) in enumerate(((owner_in, owner), (row_in, row), (col_in, col)))
    ]
    amp_load = pltpu.make_async_copy(amp_in, amp, amp_sem)
    side_loads = [
        pltpu.make_async_copy(tile.at[:, :, pl.ds(first, LANES)], sides.at[i], side_sems.at[i])
        for i, first in enumerate((0, cols - LANES))
    ]
    end_loads = [
        pltpu.make_async_copy(tile.at[:, pl.ds(first, SUBLANES), :], ends.at[i], end_sems.at[i])
        for i, first in enumerate((0, rows - SUBLANES))
    ]
    for load in int_loads + [amp_load] + end_loads + side_loads:
        load.start()
    me = lax.axis_index("pos")
    for slot in range(n_pos * capacity):
        source[slot] = 0
    for q in range(n_pos):
        counts[q] = 0
    for load in int_loads:
        load.wait()
    for item in range(pos_dev):
        who = owner[item]
        rank = counts[who]
        source[who * capacity + rank] = item
        counts[who] = rank + 1
    stores = []
    amp_load.wait()
    for d in order:
        partner = jnp.bitwise_xor(me, d)
        for k in range(capacity):
            item = source[partner * capacity + k]
            store = pltpu.make_async_copy(amp.at[item], outs[d].at[pl.ds(k * size, size)], out_sems.at[d, k])
            store.start()
            stores.append(store)
    edges[...] = jnp.zeros(edges.shape, f32)
    place = 1
    for i, lane_of_edge in enumerate((0, LANES - 1)):
        pick = (lax.broadcasted_iota(jnp.int32, (SUBLANES, LANES), 1) == lane_of_edge).astype(bf16)
        side_loads[i].wait()
        for plane in range(2):
            turned = lax.dot_general(
                pick, sides[i, plane].astype(bf16), (((1,), (1,)), ((), ())), preferred_element_type=f32
            )
            for part in range(rows // size):
                edges[place : place + 1, :] = turned[0:1, part * size : (part + 1) * size]
                place += 1
    edge_block = edges[...]
    lane = lax.broadcasted_iota(jnp.int32, (INFO_ROWS, size), 1)
    at_info = lax.broadcasted_iota(jnp.int32, (INFO_ROWS, size), 0) == 0
    for d in order:
        partner = jnp.bitwise_xor(me, d)
        held = counts[partner]
        block = jnp.zeros((INFO_ROWS, size), f32)
        for k in range(capacity):
            item = source[partner * capacity + k]
            for j, number in enumerate((row[item], col[item], (k < held).astype(jnp.int32))):
                block = jnp.where(lane == 3 * k + j, number.astype(f32), block)
        info[d] = jnp.where(at_info, block, edge_block).astype(bf16)
        store = pltpu.make_async_copy(info.at[d], outs[d].at[pl.ds(capacity * size, INFO_ROWS)], info_sems.at[d])
        store.start()
        stores.append(store)
    rim_rows[...] = jnp.zeros(rim_rows.shape, f32)
    for i, at in enumerate((0, SUBLANES - 1)):
        end_loads[i].wait()
        for plane in range(2):
            for part, first in enumerate(range(0, cols, size)):
                width = min(size, cols - first)
                place = (2 * i + plane) * rim_width(cols, size) + part
                rim_rows[place : place + 1, :width] = ends[i, plane, at : at + 1, first : first + width]
    store = pltpu.make_async_copy(rim_rows, rim, end_sems.at[2])
    store.start()
    stores.append(store)
    for store in stores:
        store.wait()


def pack(owner, row, col, amplitude, tile, n_pos, capacity, order):
    pos_dev, size, _ = amplitude.shape
    _, rows, cols = tile.shape
    far = pl.BlockSpec(memory_space=pltpu.HBM)
    ints = pltpu.SMEM((pos_dev,), jnp.int32)
    rim_shape = (-(-4 * rim_width(cols, size) // SUBLANES) * SUBLANES, size)
    return pl.pallas_call(
        functools.partial(pack_kernel, n_pos, capacity, order),
        in_specs=[far] * 5,
        out_specs=[far] * (n_pos + 1),
        out_shape=[jax.ShapeDtypeStruct((capacity * size + INFO_ROWS, size), bf16)] * n_pos
        + [jax.ShapeDtypeStruct(rim_shape, f32)],
        scratch_shapes=[
            ints,
            ints,
            ints,
            pltpu.SMEM((n_pos,), jnp.int32),
            pltpu.SMEM((n_pos * capacity,), jnp.int32),
            pltpu.VMEM(amplitude.shape, bf16),
            pltpu.VMEM((2, 2, rows, LANES), f32),
            pltpu.VMEM((2, 2, SUBLANES, cols), f32),
            pltpu.VMEM((INFO_ROWS, size), f32),
            pltpu.VMEM((n_pos, INFO_ROWS, size), bf16),
            pltpu.VMEM(rim_shape, f32),
            pltpu.SemaphoreType.DMA((3,)),
            pltpu.SemaphoreType.DMA,
            pltpu.SemaphoreType.DMA((2,)),
            pltpu.SemaphoreType.DMA((3,)),
            pltpu.SemaphoreType.DMA((n_pos, capacity)),
            pltpu.SemaphoreType.DMA((n_pos,)),
        ],
        compiler_params=pltpu.CompilerParams(vmem_limit_bytes=PACK_VMEM),
        cost_estimate=pl.CostEstimate(flops=2**20, bytes_accessed=2**20, transcendentals=0),
        name="pack",
    )(owner, row, col, amplitude, tile)


def read_info(block, count):
    lane = lax.broadcasted_iota(jnp.int32, block.shape, 1)
    first = lax.broadcasted_iota(jnp.int32, block.shape, 0) == 0
    values = block.astype(f32)
    return [jnp.sum(jnp.where(first & (lane == j), values, 0.0)).astype(jnp.int32) for j in range(count)]


def window(tile, plane, row, col, size, parts):
    shift = lax.rem(LANES - col, LANES)
    keep = lax.broadcasted_iota(jnp.int32, (size, LANES), 1) < LANES - col
    rolled = [pltpu.roll(tile[plane * parts + k, pl.ds(row, size), :], shift, 1) for k in range(size // LANES + 1)]
    return jnp.concatenate([jnp.where(keep, rolled[k], rolled[k + 1]) for k in range(size // LANES)], axis=1)


def add_window(acc, plane, row, col, value, size, parts):
    inner = size // LANES
    keep = lax.broadcasted_iota(jnp.int32, (size, LANES), 1) >= col
    zero = jnp.zeros((size, LANES), f32)
    rolled = [pltpu.roll(value[:, k * LANES : (k + 1) * LANES], lax.rem(col, LANES), 1) for k in range(inner)]
    for k in range(inner + 1):
        here = rolled[k] if k < inner else zero
        before = rolled[k - 1] if k > 0 else zero
        acc[plane * parts + k, pl.ds(row, size), :] += jnp.where(keep, here, before)


def side_by_side(stacked, size):
    return jnp.concatenate([stacked[:size], stacked[size:]], axis=1)


def buffer_terms(amp, tile, probe, left, right, emit, term_in, term, capacity, size, parts):
    numbers = read_info(amp[capacity * size :, :], 3 * capacity)
    slots = [tuple(numbers[3 * k : 3 * k + 3]) for k in range(capacity)]
    probe_re = probe[0]
    probe_im = probe[1]
    patches, psis = [], []
    for row, col, _ in slots:
        patch_re = window(tile, 0, row, col, size, parts)
        patch_im = window(tile, 1, row, col, size, parts)
        patches.append((patch_re.astype(bf16), patch_im.astype(bf16)))
        psi_re = (probe_re * patch_re - probe_im * patch_im).astype(bf16)
        psi_im = (probe_re * patch_im + probe_im * patch_re).astype(bf16)
        psis.append(jnp.concatenate([psi_re, psi_im], axis=0))
    halves = [side_by_side(dot(left[...], psi).astype(bf16), size) for psi in psis]
    waves = [dot(half, right[...]) for half in halves]
    diffs = []
    for k, wave in enumerate(waves):
        wave_re = wave[:, :size]
        wave_im = wave[:, size:]
        square = wave_re * wave_re + wave_im * wave_im
        measured = amp[k * size : (k + 1) * size, :].astype(f32)
        factor = (1.0 - measured * lax.rsqrt(jnp.maximum(square, 0.25))) * slots[k][2].astype(f32)
        diffs.append(jnp.concatenate([(wave_re * factor).astype(bf16), (wave_im * factor).astype(bf16)], axis=0))
    backs = [side_by_side(dot(right[...], diff).astype(bf16), size) for diff in diffs]
    chis = [dot(back, left[...]) for back in backs]
    sum_re = sum_im = 0.0
    for slot, ((row, col, _), (patch_re, patch_im), chi) in enumerate(zip(slots, patches, chis)):
        chi_re = chi[:, :size]
        chi_im = chi[:, size:]
        emit(slot, 0, row, col, (probe_re * chi_re + probe_im * chi_im).astype(bf16))
        emit(slot, 1, row, col, (probe_re * chi_im - probe_im * chi_re).astype(bf16))
        patch_re = patch_re.astype(f32)
        patch_im = patch_im.astype(f32)
        sum_re += patch_re * chi_re + patch_im * chi_im
        sum_im += patch_re * chi_im - patch_im * chi_re
    term[0] = term_in[0] + sum_re
    term[1] = term_in[1] + sum_im


def terms_kernel(count, capacity, first, last, probe, left, right, *rest):
    size = probe.shape[1]
    messages, rest = rest[:count], rest[count:]
    if first:
        source, tile, acc, term = rest
        parts = tile.shape[0] // 2
        for plane in range(2):
            for k in range(parts):
                block = source[plane, :, k * LANES : (k + 1) * LANES]
                tile[plane * parts + k] = block.astype(bf16).astype(f32)
        acc[...] = jnp.zeros(acc.shape, f32)
        term[...] = jnp.zeros(term.shape, f32)
        term_in = term
    elif last:
        tile, term_in, grads, keep, send, term = rest
        parts = tile.shape[0] // 2
    else:
        tile, acc_in, term_in, acc, term = rest
        parts = tile.shape[0] // 2
        acc[...] = acc_in[...]

    def emit(slot, plane, row, col, grad):
        if last:
            grads[slot, plane] = grad
        else:
            add_window(acc, plane, row, col, grad.astype(f32), size, parts)

    for message in messages:
        buffer_terms(message, tile, probe, left, right, emit, term_in, term, capacity, size, parts)
        term_in = term
    if last:
        half = size // 2
        odd = lax.rem(lax.axis_index("pos"), 2)
        keep[...] = term[:, pl.ds(pl.multiple_of(odd * half, half), half), :]
        send[...] = term[:, pl.ds(pl.multiple_of((1 - odd) * half, half), half), :]


def terms(probe, left, right, messages, capacity, source=None, state=None, last=False):
    size = probe.shape[1]
    count = len(messages)
    full = pl.BlockSpec(memory_space=pltpu.VMEM)
    scratch = []
    if state is None:
        _, rows, cols = source.shape
        blocks = jax.ShapeDtypeStruct((2 * cols // LANES, rows, LANES), f32)
        operands = (source,)
        shapes = [blocks, blocks, jax.ShapeDtypeStruct(probe.shape, f32)]
        aliases = {}
    else:
        tile, acc, term = state
        if last:
            operands = (tile, term)
            shapes = [jax.ShapeDtypeStruct((capacity, 2, size, size), bf16)]
            shapes += [jax.ShapeDtypeStruct((2, size // 2, size), f32)] * 2
            scratch = [pltpu.VMEM(term.shape, f32)]
            aliases = {}
        else:
            operands = state
            shapes = [jax.ShapeDtypeStruct(acc.shape, f32), jax.ShapeDtypeStruct(term.shape, f32)]
            aliases = {4 + count: 0, 5 + count: 1}
    results = pl.pallas_call(
        functools.partial(terms_kernel, count, capacity, state is None, last),
        in_specs=[full] * (3 + count + len(operands)),
        out_specs=[full] * len(shapes),
        out_shape=shapes,
        scratch_shapes=scratch,
        input_output_aliases=aliases,
        compiler_params=pltpu.CompilerParams(vmem_limit_bytes=TERMS_VMEM),
        cost_estimate=pl.CostEstimate(
            flops=2 * size**3 * capacity * count, bytes_accessed=2**18, transcendentals=0
        ),
        name="terms",
    )(probe, left, right, *messages, *operands)
    return tuple(results) if state is None or last else (state[0], *results)


def add_kernel(capacity, message, grads, acc_in, acc, info, sem):
    _, _, size, _ = grads.shape
    parts = acc.shape[0] // 2
    load = pltpu.make_async_copy(message.at[pl.ds(capacity * size, INFO_ROWS)], info, sem)
    load.start()
    acc[...] = acc_in[...]
    load.wait()
    numbers = read_info(info[...], 3 * capacity)
    for slot in range(capacity):
        for plane in range(2):
            add_window(acc, plane, numbers[3 * slot], numbers[3 * slot + 1], grads[slot, plane].astype(f32), size, parts)


def add_grads(message, grads, acc):
    capacity, _, size, _ = grads.shape
    full = pl.BlockSpec(memory_space=pltpu.VMEM)
    return pl.pallas_call(
        functools.partial(add_kernel, capacity),
        in_specs=[pl.BlockSpec(memory_space=pltpu.HBM), full, full],
        out_specs=full,
        out_shape=jax.ShapeDtypeStruct(acc.shape, f32),
        scratch_shapes=[pltpu.VMEM((INFO_ROWS, size), bf16), pltpu.SemaphoreType.DMA],
        input_output_aliases={2: 0},
        compiler_params=pltpu.CompilerParams(vmem_limit_bytes=SMALL_VMEM),
        cost_estimate=pl.CostEstimate(flops=2**20, bytes_accessed=2**18, transcendentals=0),
        name="add",
    )(message, grads, acc)


def finish_kernel(n_pos, n_obj, ring, steps, capacity, size, tile, acc, *rest):
    ends, rest = rest[: len(steps)], rest[len(steps) :]
    messages, (out, infos, chosen, sems) = rest[: len(ring)], rest[len(ring) :]
    loads = [
        pltpu.make_async_copy(message.at[pl.ds(capacity * size, INFO_ROWS)], infos.at[i], sems.at[i])
        for i, message in enumerate(messages)
    ]
    for load in loads:
        load.start()
    for load in loads:
        load.wait()
    _, rows, cols = tile.shape
    parts = cols // LANES
    each = rows // size
    me = lax.axis_index("pos")
    for side, neighbour in enumerate((lax.rem(me + n_pos - 1, n_pos), lax.rem(me + 1, n_pos))):
        block = jnp.zeros((INFO_ROWS, size), f32)
        for i, d in enumerate(ring):
            block = jnp.where(jnp.bitwise_xor(me, neighbour) == d, infos[i].astype(f32), block)
        chosen[side] = block

    def edge(side, plane):
        place = 1 + (2 * each if side == 0 else 0) + plane * each
        values = [chosen[side, place + i : place + i + 1, :] for i in range(each)]
        return jnp.concatenate([jnp.transpose(jnp.broadcast_to(v, (LANES, size))) for v in values], axis=0)

    level = lax.axis_index("obj")
    rim_at = 2 * size // n_pos

    def end_row(side, plane, k):
        neighbour = lax.rem(level + (n_obj - 1 if side == 0 else 1), n_obj)
        place = rim_at + (2 * (1 - side) + plane) * rim_width(cols, size) + k * LANES // size
        lanes = slice(k * LANES % size, k * LANES % size + LANES)
        value = jnp.zeros((1, LANES), f32)
        for block, step in zip(ends, steps):
            value = jnp.where(jnp.bitwise_xor(level, neighbour) == step, block[place : place + 1, lanes], value)
        return value

    lane = lax.broadcasted_iota(jnp.int32, (rows, LANES), 1)
    line = lax.broadcasted_iota(jnp.int32, (rows, LANES), 0)
    for plane in range(2):
        blocks = [tile[plane, :, k * LANES : (k + 1) * LANES] for k in range(parts)]
        to_right = [pltpu.roll(block, 1, 1) for block in blocks]
        to_left = [pltpu.roll(block, LANES - 1, 1) for block in blocks]
        low, high = edge(0, plane), edge(1, plane)
        for k in range(parts):
            here = slice(k * LANES, (k + 1) * LANES)
            block = blocks[k]
            near = jnp.where(lane == 0, to_right[k - 1] if k > 0 else low, to_right[k])
            near += jnp.where(lane == LANES - 1, to_left[k + 1] if k + 1 < parts else high, to_left[k])
            near += jnp.where(line == 0, end_row(0, plane, k), pltpu.roll(block, 1, 0))
            near += jnp.where(line == rows - 1, end_row(1, plane, k), pltpu.roll(block, rows - 1, 0))
            smooth = 4.0 * block - near
            out[plane, :, here] = block - 0.25 * (acc[plane * parts + k] + 0.5 * smooth)


def finish(tile, acc, steps, ends, ring, messages, n_pos, n_obj, capacity, size):
    full = pl.BlockSpec(memory_space=pltpu.VMEM)
    far = pl.BlockSpec(memory_space=pltpu.HBM)
    return pl.pallas_call(
        functools.partial(finish_kernel, n_pos, n_obj, ring, steps, capacity, size),
        in_specs=[full] * (2 + len(ends)) + [far] * len(ring),
        out_specs=full,
        out_shape=jax.ShapeDtypeStruct(tile.shape, f32),
        scratch_shapes=[
            pltpu.VMEM((len(ring), INFO_ROWS, size), bf16),
            pltpu.VMEM((2, INFO_ROWS, size), f32),
            pltpu.SemaphoreType.DMA((len(ring),)),
        ],
        compiler_params=pltpu.CompilerParams(vmem_limit_bytes=SMALL_VMEM),
        cost_estimate=pl.CostEstimate(flops=2**24, bytes_accessed=2**23, transcendentals=0),
        name="finish",
    )(tile, acc, *ends, *messages)


def small_call(body, name, operands, shapes):
    return pl.pallas_call(
        body,
        out_shape=shapes,
        compiler_params=pltpu.CompilerParams(vmem_limit_bytes=SMALL_VMEM),
        name=name,
    )(*operands)


def split_kernel(pairs, keep, got, *pieces):
    rows = pieces[0].shape[1]
    pair = lax.axis_index("pos") // 2
    for d in range(pairs):
        here = pl.ds(pl.multiple_of(jnp.bitwise_xor(pair, d) * rows, rows), rows)
        pieces[d][...] = keep[:, here, :] + got[:, here, :]


def join_kernel(pairs, scale, probe, *rest):
    pieces, out = rest[:pairs], rest[pairs]
    rows = pieces[0].shape[1]
    half = out.shape[1]
    me = lax.axis_index("pos")
    for d in range(pairs):
        start = jnp.bitwise_xor(me // 2, d) * rows
        old = probe[:, pl.ds(pl.multiple_of(lax.rem(me, 2) * half + start, rows), rows), :]
        out[:, pl.ds(pl.multiple_of(start, rows), rows), :] = old - pieces[d][...] * scale


def whole_kernel(mine, other, out, sems):
    half = mine.shape[1]
    odd = lax.rem(lax.axis_index("pos"), 2)
    copies = [
        pltpu.make_async_copy(value, out.at[:, pl.ds(pl.multiple_of(which * half, half), half), :], sems.at[i])
        for i, (value, which) in enumerate(((mine, odd), (other, 1 - odd)))
    ]
    for copy in copies:
        copy.start()
    for copy in copies:
        copy.wait()


def whole(mine, other):
    planes, half, size = mine.shape
    full = pl.BlockSpec(memory_space=pltpu.VMEM)
    return pl.pallas_call(
        whole_kernel,
        in_specs=[full, full],
        out_specs=pl.BlockSpec(memory_space=pltpu.HBM),
        out_shape=jax.ShapeDtypeStruct((planes, 2 * half, size), f32),
        scratch_shapes=[pltpu.SemaphoreType.DMA((2,))],
        compiler_params=pltpu.CompilerParams(vmem_limit_bytes=SMALL_VMEM),
        name="whole",
    )(mine, other)


def step_probe(probe, keep, send, scale, rim, acc, beside):
    n_pos = lax.axis_size("pos")
    n_obj = lax.axis_size("obj")
    pairs = n_pos // 2
    planes, half, size = keep.shape
    rows = half // pairs
    shape = jax.ShapeDtypeStruct((planes, rows, size), f32)
    got = exchange(send, "pos", 1)
    pieces = small_call(functools.partial(split_kernel, pairs), "split", (keep, got), [shape] * pairs)
    total = pieces[0]
    for d in reversed(range(1, pairs)):
        total = total + exchange(pieces[d], "pos", 2 * d)
    steps, ends = [], []
    while 2 ** len(steps) < n_obj:
        flat = total.reshape(planes * rows, size)
        got = exchange(jnp.concatenate([flat, rim]), "obj", 2 ** len(steps))
        if not steps:
            got, acc = lax.optimization_barrier((got, acc))
        total = total + got[: planes * rows].reshape(total.shape)
        rim = got[planes * rows :]
        steps.append(2 ** (len(steps) + 1) - 1)
        ends.append(got)
    gathered = [total] + [exchange(total, "pos", 2 * d) for d in range(1, pairs)]
    gathered, result = lax.optimization_barrier((gathered, beside(acc, steps, ends)))
    mine = small_call(
        functools.partial(join_kernel, pairs, scale),
        "join",
        (probe, *gathered),
        jax.ShapeDtypeStruct(keep.shape, f32),
    )
    other = exchange(mine, "pos", 1)
    new_probe = whole(mine, other)
    return new_probe, result


def shards(object_field, probe, amplitude, row_offset, col_offset, owner):
    n_pos = lax.axis_size("pos")
    n_obj = lax.axis_size("obj")
    pos_dev, size, _ = amplitude.shape
    capacity = max(2, pos_dev // n_pos + 1)
    left, right = (jnp.asarray(table) for table in dft_blocks(size))
    if n_pos == 8:
        early, later = [1, 2, 4, 3, 5], {4: [6], 3: [7]}
        order = [1, 0, 2, 4, 3, 5, 6, 7]
    else:
        window = 4
        order = [1, 0] + list(range(2, n_pos))
        early, later = list(range(1, 1 + window)), {d: [d + window] for d in range(1, n_pos - window)}
    *packed, rim = pack(
        owner, row_offset, col_offset, amplitude, object_field, n_pos, capacity, early + [d for d in order if d not in early]
    )
    received = {d: exchange(packed[d], "pos", d) for d in early}
    received[0] = packed[0]
    state = terms(probe, left, right, [received[order[0]]], capacity, source=object_field)
    for d in order[:-1]:
        if d != order[0]:
            state = terms(probe, left, right, [received[d]], capacity, state=state)
        for e in later.get(d, []):
            state, sending = lax.optimization_barrier((state, packed[e]))
            received[e] = exchange(sending, "pos", e)
    grads, keep, send = terms(probe, left, right, [received[order[-1]]], capacity, state=state, last=True)
    acc = add_grads(received[order[-1]], grads, state[1])
    ring = sorted({i ^ ((i + 1) % n_pos) for i in range(n_pos)})
    near = [received[d] for d in ring]

    def object_step(acc, steps, ends):
        return finish(object_field, acc, steps, ends, ring, near, n_pos, n_obj, capacity, size)

    scale = 1.0 / math.sqrt(pos_dev * n_pos * n_obj)
    new_probe, new_object = step_probe(probe, keep, send, scale, rim, acc, object_step)
    return (new_object, new_probe)


def solution(mesh):
    placed = (
        P(None, "obj", "pos"),
        P(),
        P(("pos", "obj"), None, None),
        P(("pos", "obj")),
        P(("pos", "obj")),
        P(("pos", "obj")),
    )
    return jax.shard_map(
        shards, mesh=mesh, in_specs=placed, out_specs=(P(None, "obj", "pos"), P()), check_vma=False
    )
```
